32 devices in a mesh: groups: 2 (over y), ctx: 4 (over z), dp: 2 (over x), inner: 2 (over core).
Axes of the slice: x: 2, y: 2, z: 4, core: 2. Of those that a mesh axis runs over, the one named last changes fastest.
Arguments:
- grad_out: bfloat16 [4096, 8192], P(('groups', 'ctx'), ('dp', 'inner')), parts along dimension 0, may hold values from -6 to 6
- saved_x: bfloat16 [4096, 8192], P(('groups', 'ctx'), ('dp', 'inner')), parts along dimension 0, may hold values from -6 to 6
- saved_b: bfloat16 [4096, 2048], P(('groups', 'ctx'), ('dp', 'inner')), parts along dimension 0, may hold values from -1.5 to 1.5
- saved_c: bfloat16 [4096, 2048], P(('groups', 'ctx'), ('dp', 'inner')), parts along dimension 0, may hold values from -1.5 to 1.5
- step_size: bfloat16 [4096, 128], P(('groups', 'ctx'), ('dp', 'inner')), parts along dimension 0, may hold values from 0.0055242717 to 0.022097087
- decay_rate: float32 [128], P(('dp', 'inner')), may hold values from -2.71529 to -0.022097087
- skip_gain: float32 [128], P(('dp', 'inner')), may hold values from 0.5 to 1.5
Outputs:
- grad_x: bfloat16 [4096, 8192], P(('groups', 'ctx'), ('dp', 'inner')), parts along dimension 0
- grad_b: bfloat16 [4096, 2048], P(('groups', 'ctx'), ('dp', 'inner')), parts along dimension 0
- grad_c: bfloat16 [4096, 2048], P(('groups', 'ctx'), ('dp', 'inner')), parts along dimension 0
The draws below stay inside these ranges and needn't reach their ends.
There are 2 independent parts, one for each index of `groups`. The reference program is written for one: setup_inputs(seed, part) draws one part's arguments, and reference() takes and returns one part's arrays. A program takes and returns all parts, laid end to end along the dimension named above; an argument that names none is the same for every part. Nothing has to cross between parts.
All inputs are finite; a program needn't handle non-finite values.
Results may differ from the reference program's by a relative error of at most 0.0063.
Values may be sent and summed in bfloat16 or wider, within the bound.
No kernel may reach another device: no remote copies, remote signals or barrier semaphores. Data moves between devices by JAX's collectives and lax.ppermute only.
A program may use at most 128 MiB of HBM per device.

```python
import math
from functools import partial
import jax
import jax.numpy as jnp
from jax import lax

H = 128
P_SIZE = 64
N = 256
G = 8
SEG = 256
LENGTH = 2048


def draw_step_size(key, part):
    root_len = jnp.sqrt(jnp.float32(LENGTH))
    values = jnp.exp(jax.random.uniform(key, (LENGTH, H), jnp.float32, jnp.log(0.26), jnp.log(0.98)))
    return (values / root_len).astype(jnp.bfloat16)


def draw_decay_rate(key, part):
    pick_key, slow_key, fast_key = jax.random.split(key, 3)
    root_len = jnp.sqrt(jnp.float32(LENGTH))
    fast_share = 0.5
    fast_heads = jax.random.bernoulli(pick_key, fast_share, (H,))
    slow_rate = jnp.exp(jax.random.uniform(slow_key, (H,), jnp.float32, 0.02, jnp.log(3.5))) / root_len
    fast_rate = jnp.exp(jax.random.uniform(fast_key, (H,), jnp.float32, jnp.log(0.03), jnp.log(0.059))) * root_len
    return -jnp.where(fast_heads, fast_rate, slow_rate)


def block_scale(rng, shape, cuts, least, top_value):
    level = 1.0
    for position, parts in cuts:
        draws = jax.random.uniform(jax.random.fold_in(jax.random.fold_in(rng, 6), position), (parts,), jnp.float32, least / len(cuts), top_value / len(cuts))
        level = level * jnp.repeat(jnp.exp(draws), shape[position] // parts).reshape((-1,) + (1,) * (len(shape) - 1 - position))
    return level


def scatter_about(stream_key, dims, scale, limit, cuts=(), dtype=jnp.bfloat16):
    drawn = jax.random.normal(stream_key, dims, jnp.float32) * scale
    if len(cuts) > 0:
        drawn = block_scale(stream_key, dims, cuts, -0.22, 0.18) * drawn
    return jnp.clip(drawn, min=-limit, max=limit).astype(dtype)


def setup_inputs(seed: int = 0, part: int = 0) -> dict:
    streams_of = jax.random.split(jax.random.key(seed), 8)
    part_keys = jax.random.split(jax.random.fold_in(streams_of[7], part), 8)
    return {
        "grad_out": scatter_about(part_keys[0], (LENGTH, H * P_SIZE), 1.0, 6.0, ((0, 4), (1, 4))),
        "saved_x": scatter_about(part_keys[1], (LENGTH, H * P_SIZE), 1.0, 6.0, ((0, 4), (1, 4))),
        "saved_b": scatter_about(part_keys[2], (LENGTH, G * N), 0.25, 1.5, ((0, 4), (1, 4))),
        "saved_c": scatter_about(part_keys[3], (LENGTH, G * N), 0.25, 1.5, ((0, 4), (1, 4))),
        "step_size": draw_step_size(jax.random.fold_in(jax.random.fold_in(streams_of[7], part), 71), part),
        "decay_rate": draw_decay_rate(jax.random.fold_in(streams_of[7], 71), part),
        "skip_gain": jnp.clip(0.5 + 1.0 * jax.random.uniform(streams_of[6], (H,), jnp.float32) ** block_scale(streams_of[6], (H,), ((0, 4),), -0.2, 0.2), 0.5, 1.5),
    }


def product(form, left, right):
    return jnp.einsum(form, left.astype(jnp.float32), right.astype(jnp.float32), precision=lax.Precision.HIGHEST)


def prepare(step_rows, head_rates, seg_len):
    total, groups, per_group = step_rows.shape
    as_float = step_rows.astype(jnp.float32).reshape(total // seg_len, seg_len, groups, per_group)
    step_sizes = jnp.transpose(as_float, (0, 2, 3, 1))
    cum_decay = jnp.cumsum(step_sizes * head_rates[None, :, :, None], axis=-1)
    return step_sizes, cum_decay


def summaries(grad_seg, x_seg, b_seg, c_seg, step_sizes, cum_decay):
    last_cum = cum_decay[..., -1:]
    tail_weight = jnp.moveaxis(jnp.exp(last_cum - cum_decay) * step_sizes, 3, 1)[..., None]
    head_weight = jnp.moveaxis(jnp.exp(cum_decay), 3, 1)[..., None]
    b_weighted = (tail_weight * b_seg[:, :, :, None, :].astype(jnp.float32)).astype(jnp.bfloat16)
    c_weighted = (head_weight * c_seg[:, :, :, None, :].astype(jnp.float32)).astype(jnp.bfloat16)
    fwd_local = product("ckgjp,ckgjn->cgjpn", x_seg, b_weighted)
    back_local = product("ckgjp,ckgjn->cgjpn", grad_seg, c_weighted)
    return jnp.exp(last_cum[..., 0]), fwd_local, back_local


def entering(decays, local_states, reverse):
    def advance(carry, pieces):
        running, state = carry
        decay_now, local_now = pieces
        return (running * decay_now, decay_now[..., None, None] * state + local_now), (state, running)

    start = (jnp.ones(decays.shape[1:], jnp.float32), jnp.zeros(local_states.shape[1:], jnp.float32))
    (total, final), (before, prefix) = lax.scan(advance, start, (decays, local_states), reverse=reverse)
    return before, prefix, total, final


def block_grads(pieces, head_gains):
    grad_seg, x_seg, b_seg, c_seg, step_sizes, cum_decay, fwd_in, back_in = pieces
    seg_len = grad_seg.shape[1]
    places = jnp.arange(seg_len)
    lower_mask = places[:, None] >= places[None, :]
    cum_gap = cum_decay[..., :, None] - cum_decay[..., None, :]
    seg_decay = jnp.where(lower_mask, jnp.exp(jnp.where(lower_mask, cum_gap, 0.0)), 0.0)
    scores = product("ctgn,csgn->cgts", c_seg, b_seg)
    mixing = (seg_decay * scores[:, :, None]).astype(jnp.bfloat16)
    dot_rows = product("ctgjp,csgjp->cgjts", grad_seg, x_seg)
    weighted = (seg_decay * dot_rows * step_sizes[..., None, :]).astype(jnp.bfloat16)
    x_local = product("cgjts,ctgjp->csgjp", mixing, grad_seg)
    b_local = product("cgjts,ctgn->csgjn", weighted, c_seg)
    c_local = product("cgjts,csgn->ctgjn", weighted, b_seg)
    last_cum = cum_decay[..., -1:]
    tail_weight = jnp.moveaxis(jnp.exp(last_cum - cum_decay) * step_sizes, 3, 1)[..., None]
    head_weight = jnp.moveaxis(jnp.exp(cum_decay), 3, 1)[..., None]
    step_rows = jnp.moveaxis(step_sizes, 3, 1)[..., None]
    back_half = back_in.astype(jnp.bfloat16)
    fwd_half = fwd_in.astype(jnp.bfloat16)
    x_carried = product("csgn,cgjpn->csgjp", b_seg, back_half) * tail_weight
    b_carried = product("csgjp,cgjpn->csgjn", x_seg, back_half) * tail_weight
    c_carried = product("ctgjp,cgjpn->ctgjn", grad_seg, fwd_half) * head_weight
    grad_x = (step_rows * x_local + x_carried + head_gains[:, :, None] * grad_seg.astype(jnp.float32)).astype(jnp.bfloat16)
    head_b = (b_local + b_carried).astype(jnp.bfloat16)
    head_c = (c_local + c_carried).astype(jnp.bfloat16)
    return grad_x, head_b, head_c


def run_blocks(arrays, head_gains):
    seg_count = arrays[0].shape[0]
    items = arrays[0].shape[2] * arrays[0].shape[3]
    per_turn = math.gcd(seg_count, max(1, 16 // items))
    turn_count = seg_count // per_turn
    split_up = tuple(array.reshape((turn_count, per_turn) + array.shape[1:]) for array in arrays)
    results = lax.map(partial(block_grads, head_gains=head_gains), split_up)
    return tuple(result.reshape((seg_count,) + result.shape[2:]) for result in results)


def reference(grad_out, saved_x, saved_b, saved_c, step_size, decay_rate, skip_gain):
    length = grad_out.shape[0]
    per_group = H // G
    seg_count = length // SEG

    def one_group(pieces):
        grad_rows, x_rows, b_rows, c_rows, step_rows, rate_row, gain_row = pieces
        grad_seg = grad_rows.reshape(seg_count, SEG, 1, per_group, P_SIZE)
        x_seg = x_rows.reshape(seg_count, SEG, 1, per_group, P_SIZE)
        b_seg = b_rows.reshape(seg_count, SEG, 1, N)
        c_seg = c_rows.reshape(seg_count, SEG, 1, N)
        step_sizes, cum_decay = prepare(step_rows.reshape(length, 1, per_group), rate_row.reshape(1, per_group), SEG)
        decays, fwd_local, back_local = summaries(grad_seg, x_seg, b_seg, c_seg, step_sizes, cum_decay)
        fwd_in = entering(decays, fwd_local, False)[0]
        back_in = entering(decays, back_local, True)[0]
        grad_x, head_b, head_c = run_blocks((grad_seg, x_seg, b_seg, c_seg, step_sizes, cum_decay, fwd_in, back_in), gain_row.reshape(1, per_group))
        sum_b = jnp.sum(head_b.astype(jnp.float32), axis=3).astype(jnp.bfloat16)
        sum_c = jnp.sum(head_c.astype(jnp.float32), axis=3).astype(jnp.bfloat16)
        return grad_x.reshape(length, per_group * P_SIZE), sum_b.reshape(length, N), sum_c.reshape(length, N)

    stacked = (
        jnp.moveaxis(grad_out.reshape(length, G, per_group * P_SIZE), 1, 0),
        jnp.moveaxis(saved_x.reshape(length, G, per_group * P_SIZE), 1, 0),
        jnp.moveaxis(saved_b.reshape(length, G, N), 1, 0),
        jnp.moveaxis(saved_c.reshape(length, G, N), 1, 0),
        jnp.moveaxis(step_size.reshape(length, G, per_group), 1, 0),
        decay_rate.reshape(G, per_group),
        skip_gain.reshape(G, per_group),
    )
    grad_x, grad_b, grad_c = lax.map(one_group, stacked)
    return (
        jnp.moveaxis(grad_x, 0, 1).reshape(length, H * P_SIZE),
        jnp.moveaxis(grad_b, 0, 1).reshape(length, G * N),
        jnp.moveaxis(grad_c, 0, 1).reshape(length, G * N),
    )
```

```python
from functools import partial

import jax
import jax.numpy as jnp
from jax import lax
from jax.experimental import pallas as pl
from jax.experimental.pallas import tpu as pltpu
from jax.sharding import PartitionSpec as P

P_SIZE = 64
N = 256
CHUNK = 512
CHUNK_HEADS = CHUNK // P_SIZE
F32 = jnp.float32
BF16 = jnp.bfloat16
MIB = 1024 * 1024


def dot(left, right, left_dim, right_dim):
    return lax.dot_general(
        left, right, (((left_dim,), (right_dim,)), ((), ())), preferred_element_type=F32
    )


def head_spread(pair, chunk, head_count):
    rows = lax.broadcasted_iota(jnp.int32, (2 * head_count, CHUNK), 0)
    cols = lax.broadcasted_iota(jnp.int32, (2 * head_count, CHUNK), 1)
    head = jnp.where(rows >= head_count, rows - head_count, rows)
    pick = (head == chunk * CHUNK_HEADS + cols // P_SIZE).astype(F32).astype(BF16)
    return dot(pair, pick, 1, 0)


def two_terms(value, head_count):
    high = value.astype(BF16)
    low = (value - high.astype(F32)).astype(BF16)
    lane = lax.broadcasted_iota(jnp.int32, value.shape, 1)
    return jnp.where(lane < head_count, high.astype(F32), low.astype(F32)).astype(BF16)


def local_kernel(step, rate, dy, x, b, c, dyw, xw, fwd, back, decay, wx, wd):
    chunk = pl.program_id(0)
    tokens, pair_width = step.shape
    head_count = pair_width // 2

    @pl.when(chunk == 0)
    def _():
        rows = lax.broadcasted_iota(jnp.int32, (tokens, tokens), 0)
        cols = lax.broadcasted_iota(jnp.int32, (tokens, tokens), 1)
        lower = (rows >= cols).astype(F32).astype(BF16)
        cum = dot(lower, step[...], 1, 0) * rate[...]
        wd[...] = two_terms(jnp.exp(cum), head_count)
        wx[...] = two_terms(jnp.exp(-cum) * step[...].astype(F32), head_count)

    spread_d = head_spread(wd[...], chunk, head_count)
    last = spread_d[tokens - 1 : tokens, :]
    decay[...] = last
    dyw[...] = (spread_d * dy[...].astype(F32)).astype(BF16)
    xw[...] = (head_spread(wx[...], chunk, head_count) * x[...].astype(F32)).astype(BF16)
    fwd[0] = dot(b[...], xw[...], 0, 0) * last
    back[0] = dot(c[...], dyw[...], 0, 0)


def within_kernel(dyw, xw, b, c, dy, wx, gain, grad_x, grad_b, grad_c):
    group = pl.program_id(0)
    tokens = b.shape[0]
    head_count = wx.shape[1] // 2
    rows = lax.broadcasted_iota(jnp.int32, (tokens, tokens), 0)
    cols = lax.broadcasted_iota(jnp.int32, (tokens, tokens), 1)
    lower = rows >= cols
    scores = jnp.where(lower, dot(c[...], b[...], 1, 1), 0.0).astype(BF16)
    weighted = jnp.where(lower, dot(dyw[...], xw[...], 1, 1), 0.0).astype(BF16)
    grad_b[...] = dot(weighted, c[...], 0, 0)
    grad_c[...] = dot(weighted, b[...], 1, 0)
    per_group = dyw.shape[1] // CHUNK
    for part in range(per_group):
        span = pl.ds(part * CHUNK, CHUNK)
        spread = head_spread(wx[...], group * per_group + part, head_count)
        grad_x[:, span] = spread * dot(scores, dyw[:, span], 0, 0) + gain[:, span] * dy[
            :, span
        ].astype(F32)


def carried_kernel(places, fwd_in, back_in, dyw, xw, b, decay, wx, part_x, part_b, part_c, grad_x, grad_b, grad_c, sum_b, sum_c, *, per_group):
    chunk = pl.program_id(0)
    head_count = wx.shape[1] // 2
    inside = lax.rem(chunk, per_group)

    @pl.when(inside == 0)
    def _():
        sum_b[...] = part_b[...]
        sum_c[...] = part_c[...]

    back = (back_in[0].astype(F32) * decay[...]).astype(BF16)
    spread = head_spread(wx[...], chunk, head_count)
    grad_x[...] = (part_x[...] + spread * dot(b[...], back, 1, 0)).astype(BF16)
    sum_b[...] += dot(xw[...], back, 1, 1)
    sum_c[...] += dot(dyw[...], fwd_in[0], 1, 1)

    @pl.when(inside == per_group - 1)
    def _():
        grad_b[...] = sum_b[...].astype(BF16)
        grad_c[...] = sum_c[...].astype(BF16)


def on_device(grad_out, saved_x, saved_b, saved_c, step_size, decay_rate, skip_gain):
    tokens, row_width = grad_out.shape
    head_count = step_size.shape[1]
    groups = saved_b.shape[1] // N
    chunks = row_width // CHUNK
    per_group = chunks // groups
    group_width = row_width // groups
    ranks = lax.axis_size("ctx")
    rank = lax.axis_index("ctx")
    step_pair = jnp.concatenate([step_size, step_size], axis=1)
    rate_pair = jnp.concatenate([decay_rate, decay_rate]).reshape(1, 2 * head_count)
    gain_row = jnp.repeat(skip_gain, P_SIZE).reshape(1, row_width)

    whole = pl.BlockSpec((tokens, 2 * head_count), lambda c: (0, 0))
    chunk_cols = pl.BlockSpec((tokens, CHUNK), lambda c: (0, c))
    chunk_row = pl.BlockSpec((1, CHUNK), lambda c: (0, c))
    chunk_group = pl.BlockSpec((tokens, N), lambda c: (0, c // per_group))
    chunk_state = pl.BlockSpec((1, N, CHUNK), lambda c: (c, 0, 0))
    dyw, xw, fwd_local, back_local, decay, wx = pl.pallas_call(
        local_kernel,
        grid=(chunks,),
        in_specs=[
            whole,
            pl.BlockSpec((1, 2 * head_count), lambda c: (0, 0)),
            chunk_cols,
            chunk_cols,
            chunk_group,
            chunk_group,
        ],
        out_specs=[chunk_cols, chunk_cols, chunk_state, chunk_state, chunk_row, whole],
        out_shape=[
            jax.ShapeDtypeStruct((tokens, row_width), BF16),
            jax.ShapeDtypeStruct((tokens, row_width), BF16),
            jax.ShapeDtypeStruct((chunks, N, CHUNK), F32),
            jax.ShapeDtypeStruct((chunks, N, CHUNK), F32),
            jax.ShapeDtypeStruct((1, row_width), F32),
            jax.ShapeDtypeStruct((tokens, 2 * head_count), BF16),
        ],
        scratch_shapes=[pltpu.VMEM((tokens, 2 * head_count), BF16)],
        compiler_params=pltpu.CompilerParams(vmem_limit_bytes=28 * MIB),
        cost_estimate=pl.CostEstimate(
            flops=2 * tokens * row_width * (2 * N + 512),
            bytes_accessed=12 * tokens * row_width,
            transcendentals=0,
        ),
        name="local_states",
    )(step_pair, rate_pair, grad_out, saved_x, saved_b, saved_c)

    group_cols = pl.BlockSpec((tokens, group_width), lambda g: (0, g))
    group_own = pl.BlockSpec((tokens, N), lambda g: (0, g))
    part_x, part_b, part_c = pl.pallas_call(
        within_kernel,
        grid=(groups,),
        in_specs=[
            group_cols,
            group_cols,
            group_own,
            group_own,
            group_cols,
            pl.BlockSpec((tokens, 2 * head_count), lambda g: (0, 0)),
            pl.BlockSpec((1, group_width), lambda g: (0, g)),
        ],
        out_specs=[group_cols, group_own, group_own],
        out_shape=[
            jax.ShapeDtypeStruct((tokens, row_width), F32),
            jax.ShapeDtypeStruct((tokens, groups * N), F32),
            jax.ShapeDtypeStruct((tokens, groups * N), F32),
        ],
        compiler_params=pltpu.CompilerParams(vmem_limit_bytes=28 * MIB),
        cost_estimate=pl.CostEstimate(
            flops=4 * tokens * tokens * (row_width + 2 * groups * N),
            bytes_accessed=12 * tokens * row_width,
            transcendentals=0,
        ),
        name="within_device",
    )(dyw, xw, saved_b, saved_c, grad_out, wx, gain_row)

    def at(states, place):
        place = jnp.clip(place, 0, chunks - 1)
        return lax.dynamic_index_in_dim(states, place, 0, False)

    decay_rows = decay.reshape(chunks, 1, CHUNK)
    fwd_now = jnp.zeros((N, CHUNK), BF16)
    back_now = jnp.zeros((N, CHUNK), BF16)
    fwd_got, back_got = [], []
    for turn in range(chunks + ranks - 2):
        fwd_place, back_place = turn - rank, turn - (ranks - 1 - rank)
        fwd_send = (fwd_now.astype(F32) * at(decay_rows, fwd_place) + at(fwd_local, fwd_place)).astype(BF16)
        back_send = (back_now.astype(F32) * at(decay_rows, back_place) + at(back_local, back_place)).astype(BF16)
        pairs = [(r, r + 1) for r in range(ranks - 1) if 0 <= turn - r < chunks]
        fwd_now = lax.ppermute(fwd_send, "ctx", pairs)
        back_now = lax.ppermute(back_send, "ctx", [(ranks - 1 - s, ranks - 1 - d) for s, d in pairs])
        fwd_got.append(fwd_now)
        back_got.append(back_now)
    fwd_all = jnp.stack(fwd_got)
    back_all = jnp.stack(back_got)
    places = jnp.stack([jnp.maximum(rank - 1, 0), jnp.maximum(ranks - 2 - rank, 0)]).astype(jnp.int32)
    turns = chunks + ranks - 2

    def spec(shape, index):
        return pl.BlockSpec(shape, lambda c, places: index(c))

    return pl.pallas_call(
        partial(carried_kernel, per_group=per_group),
        grid_spec=pltpu.PrefetchScalarGridSpec(
            num_scalar_prefetch=1,
            grid=(chunks,),
            in_specs=[
                pl.BlockSpec((1, N, CHUNK), lambda c, places: (jnp.minimum(c + places[0], turns - 1), 0, 0)),
                pl.BlockSpec((1, N, CHUNK), lambda c, places: (jnp.minimum(c + places[1], turns - 1), 0, 0)),
                spec((tokens, CHUNK), lambda c: (0, c)),
                spec((tokens, CHUNK), lambda c: (0, c)),
                spec((tokens, N), lambda c: (0, c // per_group)),
                spec((1, CHUNK), lambda c: (0, c)),
                spec((tokens, 2 * head_count), lambda c: (0, 0)),
                spec((tokens, CHUNK), lambda c: (0, c)),
                spec((tokens, N), lambda c: (0, c // per_group)),
                spec((tokens, N), lambda c: (0, c // per_group)),
            ],
            out_specs=[
                spec((tokens, CHUNK), lambda c: (0, c)),
                spec((tokens, N), lambda c: (0, c // per_group)),
                spec((tokens, N), lambda c: (0, c // per_group)),
            ],
            scratch_shapes=[pltpu.VMEM((tokens, N), F32), pltpu.VMEM((tokens, N), F32)],
        ),
        out_shape=[
            jax.ShapeDtypeStruct((tokens, row_width), BF16),
            jax.ShapeDtypeStruct((tokens, groups * N), BF16),
            jax.ShapeDtypeStruct((tokens, groups * N), BF16),
        ],
        compiler_params=pltpu.CompilerParams(vmem_limit_bytes=28 * MIB),
        cost_estimate=pl.CostEstimate(
            flops=6 * tokens * row_width * N,
            bytes_accessed=14 * tokens * row_width,
            transcendentals=0,
        ),
        name="carried_states",
    )(places, fwd_all, back_all, dyw, xw, saved_b, decay, wx, part_x, part_b, part_c)


def solution(mesh):
    rows_cols = P(("groups", "ctx"), ("dp", "inner"))
    return jax.shard_map(
        on_device,
        mesh=mesh,
        in_specs=(rows_cols,) * 5 + (P(("dp", "inner")),) * 2,
        out_specs=(rows_cols,) * 3,
        check_vma=False,
    )
```

```python
from functools import partial

import jax
import jax.numpy as jnp
from jax import lax
from jax.experimental import pallas as pl
from jax.experimental.pallas import tpu as pltpu
from jax.sharding import PartitionSpec as P

P_SIZE = 64
N = 256
CHUNK = 512
CHUNK_HEADS = CHUNK // P_SIZE
F32 = jnp.float32
BF16 = jnp.bfloat16
PARAMS = pltpu.CompilerParams(vmem_limit_bytes=16 * 1024 * 1024)
RELAY_PARAMS = pltpu.CompilerParams(vmem_limit_bytes=4 * 1024 * 1024)
ANYWHERE = pl.BlockSpec(memory_space=pl.ANY)
IN_VMEM = pl.BlockSpec(memory_space=pltpu.VMEM)


def dot(left, right, left_dim, right_dim):
    return lax.dot_general(
        left, right, (((left_dim,), (right_dim,)), ((), ())), preferred_element_type=F32
    )


def terms(value, count):
    parts = []
    for _ in range(count):
        part = value.astype(BF16)
        parts.append(part)
        value = value - part.astype(F32)
    return parts


def head_spread(parts, chunk):
    head_count = parts[0].shape[0]
    rows = lax.broadcasted_iota(jnp.int32, (head_count, CHUNK), 0)
    cols = lax.broadcasted_iota(jnp.int32, (head_count, CHUNK), 1)
    pick = (rows == chunk * CHUNK_HEADS + cols // P_SIZE).astype(F32).astype(BF16)
    total = dot(parts[0], pick, 0, 0)
    for part in parts[1:]:
        total += dot(part, pick, 0, 0)
    return total


def lower_mask(tokens):
    rows = lax.broadcasted_iota(jnp.int32, (tokens, tokens), 0)
    cols = lax.broadcasted_iota(jnp.int32, (tokens, tokens), 1)
    return rows >= cols


def columns(row):
    size = row.shape[1]
    rows = lax.broadcasted_iota(jnp.int32, (size, size), 0)
    cols = lax.broadcasted_iota(jnp.int32, (size, size), 1)
    return jnp.sum(jnp.where(rows == cols, row, 0.0), axis=1, keepdims=True)


def local_kernel(*refs, first, last, per_group):
    if first == 0:
        step, rate, dy, x, b, c = refs[:6]
        dyw, xw, fwd, back, decay, wd, wx, fwd_send, back_send = refs[6:15]
    else:
        wd, wx, dy, x, b, c = refs[:6]
        dyw, xw, fwd, back, decay = refs[6:11]
    dy_in, x_in, b_in, c_in, sems = refs[-5:]
    tokens = dy_in.shape[0]
    low_group = first // per_group
    copies = []
    for place, (source, target, low) in enumerate(
        (
            (dy, dy_in, first * CHUNK),
            (c, c_in, low_group * N),
            (x, x_in, first * CHUNK),
            (b, b_in, low_group * N),
        )
    ):
        copies.append(
            pltpu.make_async_copy(
                source.at[:, pl.ds(low, target.shape[1])], target, sems.at[place]
            )
        )
        copies[-1].start()
    if first == 0:
        rows = lax.broadcasted_iota(jnp.int32, (tokens, tokens), 0)
        cols = lax.broadcasted_iota(jnp.int32, (tokens, tokens), 1)
        upper = (rows <= cols).astype(F32).astype(BF16)
        cum = dot(step[...], upper, 1, 0) * columns(rate[...])
        wd[0], wd[1] = terms(jnp.exp(cum), 2)
        wx[0], wx[1] = terms(jnp.exp(-cum) * step[...].astype(F32), 2)
    for place in range(4):
        copies[place].wait()
    for chunk in range(first, last):
        span = pl.ds((chunk - first) * CHUNK, CHUNK)
        group = pl.ds((chunk // per_group - low_group) * N, N)
        spread = head_spread((wd[0], wd[1]), chunk)
        end = spread[tokens - 1 : tokens, :]
        decay[chunk - first] = end
        dyw[:, span] = (spread * dy_in[:, span].astype(F32)).astype(BF16)
        spread = head_spread((wx[0], wx[1]), chunk)
        xw[:, span] = (spread * x_in[:, span].astype(F32)).astype(BF16)
        back[chunk - first] = dot(c_in[:, group], dyw[:, span], 0, 0)
        fwd[chunk - first] = dot(b_in[:, group], xw[:, span], 0, 0) * end
    if first == 0:
        fwd_send[...] = fwd[0].astype(BF16)
        back_send[...] = back[0].astype(BF16)


def piece(refs, chunk):
    if chunk == 0:
        return refs[0][...]
    return refs[1][:, pl.ds((chunk - 1) * CHUNK, CHUNK)]


def within_kernel(*refs, group, per_group):
    dyw, xw = refs[0:2], refs[2:4]
    b, c, dy, wx, gain, grad_x, grad_b, grad_c = refs[4:]
    lower = lower_mask(b.shape[0])
    own = pl.ds(group * N, N)
    chunks = range(group * per_group, (group + 1) * per_group)
    scores = jnp.where(lower, dot(c[:, own], b[:, own], 1, 1), 0.0).astype(BF16)
    weighted = sum(dot(piece(dyw, chunk), piece(xw, chunk), 1, 1) for chunk in chunks)
    weighted = jnp.where(lower, weighted, 0.0).astype(BF16)
    grad_b[...] = dot(weighted, c[:, own], 0, 0)
    grad_c[...] = dot(weighted, b[:, own], 1, 0)
    gains = terms(jnp.broadcast_to(columns(gain[...]), (gain.shape[1], 128)), 3)
    for part, chunk in enumerate(chunks):
        spread = head_spread((wx[0], wx[1]), chunk)
        rows = dy[:, pl.ds(chunk * CHUNK, CHUNK)].astype(F32)
        skip = head_spread(gains, chunk)[0:1, :] * rows
        grad_x[:, pl.ds(part * CHUNK, CHUNK)] = (
            spread * dot(scores, piece(dyw, chunk), 0, 0) + skip
        )


def ahead(step, ranks):
    rank = lax.axis_index("ctx")
    return rank if step > 0 else ranks - 1 - rank


def relay_kernel(got, states_0, states, decay_0, decay, out, *, turn, step, ranks):
    place = turn - ahead(step, ranks)
    later = jnp.clip(place - 1, 0, states.shape[0] - 1)
    state = jnp.where(place <= 0, states_0[0], states[later])
    shrink = jnp.where(place <= 0, decay_0[0], decay[later])
    out[...] = (got[...].astype(F32) * shrink + state).astype(BF16)


def chosen(candidates, step, ranks):
    source = ahead(step, ranks) - 1
    value = candidates[0][...]
    for place in range(1, len(candidates)):
        value = jnp.where(source == place, candidates[place][...], value)
    return value


def carried_kernel(*refs, chunk, per_group, last, ranks):
    fwd_in = chosen(refs[: ranks - 1], 1, ranks)
    back_in = chosen(refs[ranks - 1 : 2 * ranks - 2], -1, ranks)
    refs = refs[2 * ranks - 2 :]
    dyw, xw, b, decay, wx, part_x, part_b, part_c = refs[:8]
    group, inside = chunk // per_group, chunk % per_group
    grad_x, grad_b, grad_c = refs[-7 if last else -5 :][:3]
    x_out = refs[-4] if last else refs[-2]
    sems = refs[-1]
    place = max(chunk - 1, 0)
    span = pl.ds(place * CHUNK, CHUNK)
    own = pl.ds(group * N, N)
    copies = []

    def send(source, target, place):
        copies.append(pltpu.make_async_copy(source, target, sems.at[place]))
        copies[-1].start()

    back = (back_in.astype(F32) * decay[place]).astype(BF16)
    spread = head_spread((wx[0], wx[1]), chunk)
    carried = spread * dot(b[:, own], back, 1, 0)
    x_out[...] = (part_x[:, pl.ds(inside * CHUNK, CHUNK)] + carried).astype(BF16)
    send(x_out, grad_x.at[:, pl.ds(chunk * CHUNK, CHUNK)], 0)
    total_b = part_b[...] + dot(xw[:, span], back, 1, 1)
    if last:
        b_out, c_out = refs[-3:-1]
        b_out[...] = total_b.astype(BF16)
        send(b_out, grad_b.at[:, own], 1)
    else:
        grad_b[...] = total_b
    total_c = part_c[...] + dot(dyw[:, span], fwd_in, 1, 1)
    if last:
        c_out[...] = total_c.astype(BF16)
        send(c_out, grad_c.at[:, own], 2)
    else:
        grad_c[...] = total_c
    for copy in copies:
        copy.wait()


def cost(flops, bytes_accessed):
    return pl.CostEstimate(flops=flops, bytes_accessed=bytes_accessed, transcendentals=0)


def on_device(grad_out, saved_x, saved_b, saved_c, step_size, decay_rate, skip_gain):
    tokens, row_width = grad_out.shape
    head_count = step_size.shape[1]
    groups = saved_b.shape[1] // N
    chunks = row_width // CHUNK
    per_group = chunks // groups
    group_width = row_width // groups
    ranks = lax.axis_size("ctx")
    rate_row = decay_rate.reshape(1, head_count)
    gain_row = skip_gain.reshape(1, head_count)
    stay = partial(pltpu.with_memory_space_constraint, memory_space=pltpu.HBM)
    sources = [stay(array) for array in (grad_out, saved_x, saved_b, saved_c)]

    weight_shapes = [pltpu.VMEM((2, head_count, tokens), BF16)] * 2
    send_shapes = [jax.ShapeDtypeStruct((N, CHUNK), BF16)] * 2

    def local_states(first, last, inputs, extra_shapes):
        wide = (last - first) * CHUNK
        out_shape = [
            pltpu.VMEM((tokens, wide), BF16),
            pltpu.VMEM((tokens, wide), BF16),
            pltpu.VMEM((last - first, N, CHUNK), F32),
            pltpu.VMEM((last - first, N, CHUNK), F32),
            pltpu.VMEM((last - first, 1, CHUNK), F32),
        ] + extra_shapes
        tall = ((last - 1) // per_group - first // per_group + 1) * N
        return pl.pallas_call(
            partial(local_kernel, first=first, last=last, per_group=per_group),
            in_specs=[IN_VMEM] * 2 + [ANYWHERE] * 4,
            out_specs=[IN_VMEM] * len(out_shape),
            out_shape=out_shape,
            scratch_shapes=[
                pltpu.VMEM((tokens, wide), BF16),
                pltpu.VMEM((tokens, wide), BF16),
                pltpu.VMEM((tokens, tall), BF16),
                pltpu.VMEM((tokens, tall), BF16),
                pltpu.SemaphoreType.DMA((4,)),
            ],
            compiler_params=PARAMS,
            cost_estimate=cost(4 * tokens * wide * (N + 512), 6 * tokens * wide),
            name=f"states_{first}",
        )(*inputs)

    *head, wd, wx, fwd_send, back_send = local_states(
        0, 1, [step_size.T, rate_row] + sources, weight_shapes + send_shapes
    )
    tail = local_states(1, chunks, [wd, wx] + sources, [])

    def within(group, wx):
        return pl.pallas_call(
            partial(within_kernel, group=group, per_group=per_group),
            in_specs=[IN_VMEM] * 9,
            out_specs=[IN_VMEM] * 3,
            out_shape=[
                pltpu.VMEM((tokens, group_width), F32),
                pltpu.VMEM((tokens, N), F32),
                pltpu.VMEM((tokens, N), F32),
            ],
            compiler_params=PARAMS,
            cost_estimate=cost(
                4 * tokens * tokens * (group_width + 2 * N), 10 * tokens * group_width
            ),
            name=f"within_{group}",
        )(head[0], tail[0], head[1], tail[1], saved_b, saved_c, grad_out, wx, gain_row)

    def relay(turn, step, got):
        kind = 2 if step > 0 else 3
        return pl.pallas_call(
            partial(relay_kernel, turn=turn, step=step, ranks=ranks),
            in_specs=[IN_VMEM] * 5,
            out_specs=IN_VMEM,
            out_shape=pltpu.VMEM((N, CHUNK), BF16),
            compiler_params=RELAY_PARAMS,
            cost_estimate=cost(4 * N * CHUNK, 8 * N * CHUNK),
            name=f"relay_{turn}_{kind}",
        )(got, head[kind], tail[kind], head[4], tail[4])

    def carried(chunk, fwd_in, back_in, part_x, part_b, part_c, grads):
        own = head if chunk == 0 else tail
        last = chunk % per_group == per_group - 1
        out_shape = [jax.ShapeDtypeStruct((tokens, row_width), BF16)]
        out_specs = [ANYWHERE]
        scratch = [pltpu.VMEM((tokens, CHUNK), BF16)]
        if last:
            out_shape += [jax.ShapeDtypeStruct((tokens, groups * N), BF16)] * 2
            out_specs += [ANYWHERE] * 2
            scratch += [pltpu.VMEM((tokens, N), BF16)] * 2
        else:
            out_shape += [pltpu.VMEM((tokens, N), F32)] * 2
            out_specs += [IN_VMEM] * 2
        inputs = [*fwd_in, *back_in, own[0], own[1], saved_b, own[4], wx, part_x, part_b, part_c]
        aliases = {}
        if grads[0] is not None:
            aliases[len(inputs)] = 0
            inputs.append(grads[0])
        if last and grads[1] is not None:
            for place in (1, 2):
                aliases[len(inputs)] = place
                inputs.append(grads[place])
        results = pl.pallas_call(
            partial(
                carried_kernel, chunk=chunk, per_group=per_group, last=last, ranks=ranks
            ),
            in_specs=[IN_VMEM] * (2 * ranks + 6) + [ANYWHERE] * len(aliases),
            out_specs=out_specs,
            out_shape=out_shape,
            scratch_shapes=scratch + [pltpu.SemaphoreType.DMA((3,))],
            input_output_aliases=aliases,
            compiler_params=PARAMS,
            cost_estimate=cost(6 * tokens * CHUNK * N, 14 * tokens * CHUNK),
            name=f"carried_{chunk}",
        )(*inputs)
        if last:
            return None, list(results)
        return results[1:], [results[0]] + list(grads[1:])

    fwd_got, back_got, parts = [], [], {}
    sums, grads = None, [None, None, None]
    turns = chunks + ranks - 2
    for turn in range(turns + 1):
        if 0 < turn < turns:
            fwd_send = relay(turn, 1, fwd_got[-1])
            back_send = relay(turn, -1, back_got[-1])
        if turn < turns:
            pairs = [(r, r + 1) for r in range(ranks - 1) if 0 <= turn - r < chunks]
            fwd_now = lax.ppermute(fwd_send, "ctx", pairs)
            back_now = lax.ppermute(
                back_send, "ctx", [(ranks - 1 - s, ranks - 1 - d) for s, d in pairs]
            )
        for group in range(groups):
            if turn == 1 + group:
                wx_now = lax.optimization_barrier((wx, fwd_got[-1], back_got[-1]))[0]
                parts[group] = within(group, wx_now)
                fwd_now, parts[group] = lax.optimization_barrier((fwd_now, parts[group]))
        chunk = turn - (ranks - 1)
        if 0 <= chunk < chunks:
            fwd_in = fwd_got[chunk : chunk + ranks - 1]
            back_in = back_got[chunk : chunk + ranks - 1]
            part_x, part_b, part_c = parts[chunk // per_group]
            if chunk % per_group > 0:
                part_b, part_c = sums
            sums, grads = carried(chunk, fwd_in, back_in, part_x, part_b, part_c, grads)
            if turn < turns:
                grads[0], fwd_now = lax.optimization_barrier((grads[0], fwd_now))
        fwd_got.append(fwd_now)
        back_got.append(back_now)
    return tuple(grads)


def solution(mesh):
    rows_cols = P(("groups", "ctx"), ("dp", "inner"))
    return jax.shard_map(
        on_device,
        mesh=mesh,
        in_specs=(rows_cols,) * 5 + (P(("dp", "inner")),) * 2,
        out_specs=(rows_cols,) * 3,
        check_vma=False,
    )
```

```python
from functools import partial

import jax
import jax.numpy as jnp
from jax import lax
from jax.experimental import pallas as pl
from jax.experimental.pallas import tpu as pltpu
from jax.sharding import PartitionSpec as P

P_SIZE = 64
N = 256
CHUNK = 512
CHUNK_HEADS = CHUNK // P_SIZE
F32 = jnp.float32
BF16 = jnp.bfloat16
PARAMS = pltpu.CompilerParams(vmem_limit_bytes=16 * 1024 * 1024)
RELAY_PARAMS = pltpu.CompilerParams(vmem_limit_bytes=4 * 1024 * 1024)
ANYWHERE = pl.BlockSpec(memory_space=pl.ANY)
IN_VMEM = pl.BlockSpec(memory_space=pltpu.VMEM)


def dot(left, right, left_dim, right_dim):
    return lax.dot_general(
        left, right, (((left_dim,), (right_dim,)), ((), ())), preferred_element_type=F32
    )


def terms(value, count):
    parts = []
    for _ in range(count):
        part = value.astype(BF16)
        parts.append(part)
        value = value - part.astype(F32)
    return parts


def head_spread(parts, chunk):
    head_count = parts[0].shape[0]
    rows = lax.broadcasted_iota(jnp.int32, (head_count, CHUNK), 0)
    cols = lax.broadcasted_iota(jnp.int32, (head_count, CHUNK), 1)
    pick = (rows == chunk * CHUNK_HEADS + cols // P_SIZE).astype(F32).astype(BF16)
    total = dot(parts[0], pick, 0, 0)
    for part in parts[1:]:
        total += dot(part, pick, 0, 0)
    return total


def lower_mask(tokens):
    rows = lax.broadcasted_iota(jnp.int32, (tokens, tokens), 0)
    cols = lax.broadcasted_iota(jnp.int32, (tokens, tokens), 1)
    return rows >= cols


def columns(row):
    size = row.shape[1]
    rows = lax.broadcasted_iota(jnp.int32, (size, size), 0)
    cols = lax.broadcasted_iota(jnp.int32, (size, size), 1)
    return jnp.sum(jnp.where(rows == cols, row, 0.0), axis=1, keepdims=True)


def heading(even_links, ranks):
    rank = lax.axis_index("ctx")
    forward = (lax.rem(rank, 2) == 0) == even_links
    return forward, jnp.where(forward, rank, ranks - 1 - rank)


def local_kernel(*refs, first, last, per_group, ranks):
    if first == 0:
        step_hbm, rate_hbm, dy, x, b, c = refs[:6]
        dyw, xw, states, decay, wd, wx, send = refs[6:13]
        step, rate, dy_in, x_in, b_in, c_in, sems = refs[13:]
    else:
        wd, wx, dy, x, b, c = refs[:6]
        dyw, xw, states, decay = refs[6:10]
        dy_in, x_in, b_in, c_in, sems = refs[10:]
    tokens = dy_in.shape[0]
    low_group = first // per_group

    def fetch(source, target, place):
        copy = pltpu.make_async_copy(source, target, sems.at[place])
        copy.start()
        return copy

    def part(source, target, low, place):
        return fetch(source.at[:, pl.ds(low, target.shape[1])], target, place)

    if first == 0:
        small = [fetch(step_hbm, step, 4), fetch(rate_hbm, rate, 5)]
    copies = [
        part(dy, dy_in, first * CHUNK, 0),
        part(c, c_in, low_group * N, 1),
        part(x, x_in, first * CHUNK, 2),
        part(b, b_in, low_group * N, 3),
    ]
    if first == 0:
        rows = lax.broadcasted_iota(jnp.int32, (tokens, tokens), 0)
        cols = lax.broadcasted_iota(jnp.int32, (tokens, tokens), 1)
        upper = (rows <= cols).astype(F32).astype(BF16)
        for copy in small:
            copy.wait()
        cum = dot(step[...], upper, 1, 0) * columns(rate[...])
        wd[0], wd[1] = terms(jnp.exp(cum), 2)
        wx[0], wx[1] = terms(jnp.exp(-cum) * step[...].astype(F32), 2)
    for copy in copies:
        copy.wait()
    for chunk in range(first, last):
        place = chunk - first
        span = pl.ds(place * CHUNK, CHUNK)
        group = pl.ds((chunk // per_group - low_group) * N, N)
        spread = head_spread((wd[0], wd[1]), chunk)
        end = spread[tokens - 1 : tokens, :]
        decay[place] = end
        dyw[:, span] = (spread * dy_in[:, span].astype(F32)).astype(BF16)
        spread = head_spread((wx[0], wx[1]), chunk)
        xw[:, span] = (spread * x_in[:, span].astype(F32)).astype(BF16)
        states[place, 1] = dot(c_in[:, group], dyw[:, span], 0, 0)
        states[place, 0] = dot(b_in[:, group], xw[:, span], 0, 0) * end
    if first == 0:
        forward, _ = heading(True, ranks)
        send[...] = states[0, jnp.where(forward, 0, 1)].astype(BF16)


def piece(refs, chunk, starts):
    place = max(i for i, start in enumerate(starts) if start <= chunk)
    return refs[place][:, pl.ds((chunk - starts[place]) * CHUNK, CHUNK)]


def within_kernel(*refs, group, per_group, starts):
    count = len(starts)
    dyw, xw, refs = refs[:count], refs[count : 2 * count], refs[2 * count :]
    b, c, dy, wx, gain, grad_x, grad_b, grad_c = refs
    lower = lower_mask(b.shape[0])
    own = pl.ds(group * N, N)
    chunks = range(group * per_group, (group + 1) * per_group)
    scores = jnp.where(lower, dot(c[:, own], b[:, own], 1, 1), 0.0).astype(BF16)
    weighted = sum(
        dot(piece(dyw, chunk, starts), piece(xw, chunk, starts), 1, 1) for chunk in chunks
    )
    weighted = jnp.where(lower, weighted, 0.0).astype(BF16)
    grad_b[...] = dot(weighted, c[:, own], 0, 0)
    grad_c[...] = dot(weighted, b[:, own], 1, 0)
    gains = terms(jnp.broadcast_to(columns(gain[...]), (gain.shape[1], 128)), 3)
    for part, chunk in enumerate(chunks):
        spread = head_spread((wx[0], wx[1]), chunk)
        rows = dy[:, pl.ds(chunk * CHUNK, CHUNK)].astype(F32)
        skip = head_spread(gains, chunk)[0:1, :] * rows
        grad_x[:, pl.ds(part * CHUNK, CHUNK)] = (
            spread * dot(scores, piece(dyw, chunk, starts), 0, 0) + skip
        )


def relay_kernel(*refs, turn, even_links, ranks, starts):
    out, refs = refs[-1], refs[:-1]
    count = len(starts)
    states, decays, got = refs[:count], refs[count : 2 * count], refs[2 * count :]
    forward, lag = heading(even_links, ranks)
    kind = jnp.where(forward, 0, 1)
    chunk = turn - lag
    state = shrink = None
    for start, state_ref, decay_ref in zip(starts, states, decays):
        place = jnp.clip(chunk - start, 0, state_ref.shape[0] - 1)
        if state is None:
            state, shrink = state_ref[place, kind], decay_ref[place]
        else:
            state = jnp.where(chunk >= start, state_ref[place, kind], state)
            shrink = jnp.where(chunk >= start, decay_ref[place], shrink)
    if got:
        state = got[0][...].astype(F32) * shrink + state
    out[...] = state.astype(BF16)


def chosen(candidates, source):
    value = jnp.zeros(candidates[0].shape, BF16)
    for place, candidate in enumerate(candidates):
        value = jnp.where(source == place, candidate[...], value)
    return value


def carried_kernel(*refs, chunk, per_group, last, ranks, start):
    rank = lax.axis_index("ctx")
    fwd_in = chosen(refs[: ranks - 1], rank - 1)
    back_in = chosen(refs[: ranks - 1], ranks - 2 - rank)
    refs = refs[ranks - 1 :]
    dyw, xw, b, decay, wx, part_x, part_b, part_c = refs[:8]
    group, inside = chunk // per_group, chunk % per_group
    grad_x, grad_b, grad_c = refs[-7 if last else -5 :][:3]
    x_out = refs[-4] if last else refs[-2]
    sems = refs[-1]
    place = chunk - start
    span = pl.ds(place * CHUNK, CHUNK)
    own = pl.ds(group * N, N)
    copies = []

    def send(source, target, place):
        copies.append(pltpu.make_async_copy(source, target, sems.at[place]))
        copies[-1].start()

    back = (back_in.astype(F32) * decay[place]).astype(BF16)
    spread = head_spread((wx[0], wx[1]), chunk)
    carried = spread * dot(b[:, own], back, 1, 0)
    x_out[...] = (part_x[:, pl.ds(inside * CHUNK, CHUNK)] + carried).astype(BF16)
    send(x_out, grad_x.at[:, pl.ds(chunk * CHUNK, CHUNK)], 0)
    total_b = part_b[...] + dot(xw[:, span], back, 1, 1)
    if last:
        b_out, c_out = refs[-3:-1]
        b_out[...] = total_b.astype(BF16)
        send(b_out, grad_b.at[:, own], 1)
    else:
        grad_b[...] = total_b
    total_c = part_c[...] + dot(dyw[:, span], fwd_in, 1, 1)
    if last:
        c_out[...] = total_c.astype(BF16)
        send(c_out, grad_c.at[:, own], 2)
    else:
        grad_c[...] = total_c
    for copy in copies:
        copy.wait()


def cost(flops, bytes_accessed):
    return pl.CostEstimate(flops=flops, bytes_accessed=bytes_accessed, transcendentals=0)


def on_device(grad_out, saved_x, saved_b, saved_c, step_size, decay_rate, skip_gain):
    tokens, row_width = grad_out.shape
    head_count = step_size.shape[1]
    groups = saved_b.shape[1] // N
    chunks = row_width // CHUNK
    per_group = chunks // groups
    group_width = row_width // groups
    ranks = lax.axis_size("ctx")
    gain_row = skip_gain.reshape(1, head_count)
    stay = partial(pltpu.with_memory_space_constraint, memory_space=pltpu.HBM)
    sources = [stay(array) for array in (grad_out, saved_x, saved_b, saved_c)]
    starts = [start for start in (0, 1) if start < chunks]
    stops = starts[1:] + [chunks]

    def local_states(first, last, inputs, in_spec, extra_shapes, extra_scratch):
        wide = (last - first) * CHUNK
        out_shape = [
            pltpu.VMEM((tokens, wide), BF16),
            pltpu.VMEM((tokens, wide), BF16),
            pltpu.VMEM((last - first, 2, N, CHUNK), F32),
            pltpu.VMEM((last - first, 1, CHUNK), F32),
        ] + extra_shapes
        tall = ((last - 1) // per_group - first // per_group + 1) * N
        return pl.pallas_call(
            partial(local_kernel, first=first, last=last, per_group=per_group, ranks=ranks),
            in_specs=[in_spec] * 2 + [ANYWHERE] * 4,
            out_specs=[IN_VMEM] * len(out_shape),
            out_shape=out_shape,
            scratch_shapes=extra_scratch
            + [
                pltpu.VMEM((tokens, wide), BF16),
                pltpu.VMEM((tokens, wide), BF16),
                pltpu.VMEM((tokens, tall), BF16),
                pltpu.VMEM((tokens, tall), BF16),
                pltpu.SemaphoreType.DMA((6,)),
            ],
            compiler_params=PARAMS,
            cost_estimate=cost(4 * tokens * wide * (N + 512), 6 * tokens * wide),
            name=f"states_{first}",
        )(*inputs)

    *head, wd, wx, first_send = local_states(
        0,
        stops[0],
        [stay(step_size.T), stay(decay_rate.reshape(1, head_count))] + sources,
        ANYWHERE,
        [pltpu.VMEM((2, head_count, tokens), BF16)] * 2 + [pltpu.VMEM((N, CHUNK), BF16)],
        [pltpu.VMEM((head_count, tokens), BF16), pltpu.VMEM((1, head_count), F32)],
    )
    pieces = [head]

    def more_states(wd):
        place = len(pieces)
        pieces.append(
            local_states(
                starts[place], stops[place], [wd, wx] + sources, IN_VMEM, [], []
            )
        )

    def within(group, wx):
        return pl.pallas_call(
            partial(within_kernel, group=group, per_group=per_group, starts=starts),
            in_specs=[IN_VMEM] * (2 * len(starts) + 5),
            out_specs=[IN_VMEM] * 3,
            out_shape=[
                pltpu.VMEM((tokens, group_width), F32),
                pltpu.VMEM((tokens, N), F32),
                pltpu.VMEM((tokens, N), F32),
            ],
            compiler_params=PARAMS,
            cost_estimate=cost(
                4 * tokens * tokens * (group_width + 2 * N), 10 * tokens * group_width
            ),
            name=f"within_{group}",
        )(
            *[piece[0] for piece in pieces],
            *[piece[1] for piece in pieces],
            saved_b,
            saved_c,
            grad_out,
            wx,
            gain_row,
        )

    def relay(turn, even_links, got):
        top = turn if even_links else turn - 1
        count = sum(start <= top for start in starts)
        got = [] if got is None else [got]
        return pl.pallas_call(
            partial(
                relay_kernel,
                turn=turn,
                even_links=even_links,
                ranks=ranks,
                starts=starts[:count],
            ),
            in_specs=[IN_VMEM] * (2 * count + len(got)),
            out_specs=IN_VMEM,
            out_shape=pltpu.VMEM((N, CHUNK), BF16),
            compiler_params=RELAY_PARAMS,
            cost_estimate=cost(4 * N * CHUNK, 8 * N * CHUNK),
            name=f"relay_{turn}",
        )(
            *[piece[2] for piece in pieces[:count]],
            *[piece[3] for piece in pieces[:count]],
            *got,
        )

    def carried(chunk, candidates, part_x, part_b, part_c, grads):
        place = max(i for i, start in enumerate(starts) if start <= chunk)
        own = pieces[place]
        last = chunk % per_group == per_group - 1
        out_shape = [jax.ShapeDtypeStruct((tokens, row_width), BF16)]
        out_specs = [ANYWHERE]
        scratch = [pltpu.VMEM((tokens, CHUNK), BF16)]
        if last:
            out_shape += [jax.ShapeDtypeStruct((tokens, groups * N), BF16)] * 2
            out_specs += [ANYWHERE] * 2
            scratch += [pltpu.VMEM((tokens, N), BF16)] * 2
        else:
            out_shape += [pltpu.VMEM((tokens, N), F32)] * 2
            out_specs += [IN_VMEM] * 2
        inputs = [*candidates, own[0], own[1], saved_b, own[3], wx, part_x, part_b, part_c]
        aliases = {}
        if grads[0] is not None:
            aliases[len(inputs)] = 0
            inputs.append(grads[0])
        if last and grads[1] is not None:
            for slot in (1, 2):
                aliases[len(inputs)] = slot
                inputs.append(grads[slot])
        results = pl.pallas_call(
            partial(
                carried_kernel,
                chunk=chunk,
                per_group=per_group,
                last=last,
                ranks=ranks,
                start=starts[place],
            ),
            in_specs=[IN_VMEM] * (ranks + 7) + [ANYWHERE] * len(aliases),
            out_specs=out_specs,
            out_shape=out_shape,
            scratch_shapes=scratch + [pltpu.SemaphoreType.DMA((3,))],
            input_output_aliases=aliases,
            compiler_params=PARAMS,
            cost_estimate=cost(6 * tokens * CHUNK * N, 14 * tokens * CHUNK),
            name=f"carried_{chunk}",
        )(*inputs)
        if last:
            return None, list(results)
        return results[1:], [results[0]] + list(grads[1:])

    def links(turn, even_links):
        pairs = []
        for low in range(0 if even_links else 1, ranks - 1, 2):
            if 0 <= turn - low < chunks:
                pairs.append((low, low + 1))
            if 0 <= turn - (ranks - 2 - low) < chunks:
                pairs.append((low + 1, low))
        return pairs

    turns = chunks + ranks - 2
    order = []
    for base in range(turns):
        for turn in (base, base + 1):
            even_links = base % 2 == 0
            if turn < turns and links(turn, even_links):
                order.append((turn, even_links))
    got, parts = {}, {}
    sums, grads = None, [None, None, None]
    groups_left, chunks_left = list(range(groups)), list(range(chunks))

    def carry():
        nonlocal sums, grads
        chunk = chunks_left.pop(0)
        candidates = [got[chunk + hop, hop % 2 == 0] for hop in range(ranks - 1)]
        part_x, part_b, part_c = parts[chunk // per_group]
        if chunk % per_group > 0:
            part_b, part_c = sums
        sums, grads = carried(chunk, candidates, part_x, part_b, part_c, grads)

    for position, (turn, even_links) in enumerate(order):
        before = got.get((turn - 1, not even_links))
        if position == 1 and len(pieces) < len(starts):
            more_states(wd)
        send = first_send if position == 0 else relay(turn, even_links, before)
        key = (turn, even_links)
        got[key] = lax.ppermute(send, "ctx", links(turn, even_links))
        ready = order[: position - 1]
        following = order[position - 1] if position else None
        if position == 1:
            while len(pieces) < len(starts):
                more_states(lax.optimization_barrier((wd, send))[0])
                pieces[-1], got[following] = lax.optimization_barrier(
                    (pieces[-1], got[following])
                )
        elif position % 2 == 0 and position > 0:
            if groups_left:
                group = groups_left.pop(0)
                parts[group] = within(group, lax.optimization_barrier((wx, before))[0])
                parts[group], got[following] = lax.optimization_barrier(
                    (parts[group], got[following])
                )
            elif chunks_left and (chunks_left[0] + ranks - 2, True) in ready:
                carry()
                grads[0], got[following] = lax.optimization_barrier((grads[0], got[following]))
    while groups_left:
        group = groups_left.pop(0)
        parts[group] = within(group, wx)
    while chunks_left:
        carry()
    return tuple(grads)


def solution(mesh):
    rows_cols = P(("groups", "ctx"), ("dp", "inner"))
    return jax.shard_map(
        on_device,
        mesh=mesh,
        in_specs=(rows_cols,) * 5 + (P(("dp", "inner")),) * 2,
        out_specs=(rows_cols,) * 3,
        check_vma=False,
    )
```

```python
from functools import partial

import jax
import jax.numpy as jnp
from jax import lax
from jax.experimental import pallas as pl
from jax.experimental.pallas import tpu as pltpu
from jax.sharding import PartitionSpec as P

P_SIZE = 64
N = 256
CHUNK = 512
CHUNK_HEADS = CHUNK // P_SIZE
F32 = jnp.float32
BF16 = jnp.bfloat16
PARAMS = pltpu.CompilerParams(vmem_limit_bytes=16 * 1024 * 1024)
RELAY_PARAMS = pltpu.CompilerParams(vmem_limit_bytes=4 * 1024 * 1024)
ANYWHERE = pl.BlockSpec(memory_space=pl.ANY)
IN_VMEM = pl.BlockSpec(memory_space=pltpu.VMEM)


def dot(left, right, left_dim, right_dim):
    return lax.dot_general(
        left, right, (((left_dim,), (right_dim,)), ((), ())), preferred_element_type=F32
    )


def terms(value, count):
    parts = []
    for _ in range(count):
        part = value.astype(BF16)
        parts.append(part)
        value = value - part.astype(F32)
    return parts


def head_spread(parts, chunk):
    head_count = parts[0].shape[0]
    rows = lax.broadcasted_iota(jnp.int32, (head_count, CHUNK), 0)
    cols = lax.broadcasted_iota(jnp.int32, (head_count, CHUNK), 1)
    pick = (rows == chunk * CHUNK_HEADS + cols // P_SIZE).astype(F32).astype(BF16)
    total = dot(parts[0], pick, 0, 0)
    for part in parts[1:]:
        total += dot(part, pick, 0, 0)
    return total


def lower_mask(tokens):
    rows = lax.broadcasted_iota(jnp.int32, (tokens, tokens), 0)
    cols = lax.broadcasted_iota(jnp.int32, (tokens, tokens), 1)
    return rows >= cols


def columns(row):
    size = row.shape[1]
    rows = lax.broadcasted_iota(jnp.int32, (size, size), 0)
    cols = lax.broadcasted_iota(jnp.int32, (size, size), 1)
    return jnp.sum(jnp.where(rows == cols, row, 0.0), axis=1, keepdims=True)


def heading(even_links, ranks):
    rank = lax.axis_index("ctx")
    forward = (lax.rem(rank, 2) == 0) == even_links
    return forward, jnp.where(forward, rank, ranks - 1 - rank)


def upper_ones(tokens):
    rows = lax.broadcasted_iota(jnp.int32, (tokens, tokens), 0)
    cols = lax.broadcasted_iota(jnp.int32, (tokens, tokens), 1)
    return (rows <= cols).astype(F32).astype(BF16)


def first_kernel(step_hbm, rate_hbm, dy, x, b, c, send, step, rate, rows_in, group_in, sems, *, ranks):
    rank = lax.axis_index("ctx")

    def fetch(source, target, place):
        if source.shape != target.shape:
            source = source.at[:, pl.ds(0, target.shape[1])]
        copy = pltpu.make_async_copy(source, target, sems.at[place])
        copy.start()
        return copy

    def state(wide, narrow, weigh):
        copies = [
            fetch(step_hbm, step, 0),
            fetch(rate_hbm, rate, 1),
            fetch(wide, rows_in, 2),
            fetch(narrow, group_in, 3),
        ]
        upper = upper_ones(step.shape[1])
        copies[0].wait()
        copies[1].wait()
        cum = dot(step[...], upper, 1, 0) * columns(rate[...])
        spread = head_spread(terms(weigh(cum), 2), 0)
        copies[2].wait()
        rows = (spread * rows_in[...].astype(F32)).astype(BF16)
        copies[3].wait()
        send[...] = dot(group_in[...], rows, 0, 0).astype(BF16)

    @pl.when(rank == 0)
    def _():
        state(x, b, lambda cum: jnp.exp(cum[:, -1:] - cum) * step[...].astype(F32))

    @pl.when(rank == ranks - 1)
    def _():
        state(dy, c, jnp.exp)


def local_kernel(*refs, first, last, per_group):
    if first == 0:
        step_hbm, rate_hbm, dy, x, b, c = refs[:6]
        dyw, xw, states, decay, wd, wx = refs[6:12]
        step, rate, dy_in, x_in, b_in, c_in, sems = refs[12:]
    else:
        wd, wx, dy, x, b, c = refs[:6]
        dyw, xw, states, decay = refs[6:10]
        dy_in, x_in, b_in, c_in, sems = refs[10:]
    tokens = dy_in.shape[0]
    low_group = first // per_group

    def fetch(source, target, place):
        copy = pltpu.make_async_copy(source, target, sems.at[place])
        copy.start()
        return copy

    def part(source, target, low, place):
        return fetch(source.at[:, pl.ds(low, target.shape[1])], target, place)

    if first == 0:
        small = [fetch(step_hbm, step, 4), fetch(rate_hbm, rate, 5)]
    copies = [
        part(dy, dy_in, first * CHUNK, 0),
        part(c, c_in, low_group * N, 1),
        part(x, x_in, first * CHUNK, 2),
        part(b, b_in, low_group * N, 3),
    ]
    if first == 0:
        upper = upper_ones(tokens)
        for copy in small:
            copy.wait()
        cum = dot(step[...], upper, 1, 0) * columns(rate[...])
        wd[0], wd[1] = terms(jnp.exp(cum), 2)
        wx[0], wx[1] = terms(jnp.exp(-cum) * step[...].astype(F32), 2)
    for copy in copies:
        copy.wait()
    for chunk in range(first, last):
        place = chunk - first
        span = pl.ds(place * CHUNK, CHUNK)
        group = pl.ds((chunk // per_group - low_group) * N, N)
        spread = head_spread((wd[0], wd[1]), chunk)
        end = spread[tokens - 1 : tokens, :]
        decay[place] = end
        dyw[:, span] = (spread * dy_in[:, span].astype(F32)).astype(BF16)
        spread = head_spread((wx[0], wx[1]), chunk)
        xw[:, span] = (spread * x_in[:, span].astype(F32)).astype(BF16)
        states[place, 1] = dot(c_in[:, group], dyw[:, span], 0, 0)
        states[place, 0] = dot(b_in[:, group], xw[:, span], 0, 0) * end


def piece(refs, chunk, starts):
    place = max(i for i, start in enumerate(starts) if start <= chunk)
    return refs[place][:, pl.ds((chunk - starts[place]) * CHUNK, CHUNK)]


def within_kernel(*refs, group, per_group, starts):
    count = len(starts)
    dyw, xw, refs = refs[:count], refs[count : 2 * count], refs[2 * count :]
    b, c, dy, wx, gain, grad_x, grad_b, grad_c, spread_out = refs
    lower = lower_mask(b.shape[0])
    own = pl.ds(group * N, N)
    chunks = range(group * per_group, (group + 1) * per_group)
    scores = jnp.where(lower, dot(c[:, own], b[:, own], 1, 1), 0.0).astype(BF16)
    weighted = sum(
        dot(piece(dyw, chunk, starts), piece(xw, chunk, starts), 1, 1) for chunk in chunks
    )
    weighted = jnp.where(lower, weighted, 0.0).astype(BF16)
    grad_b[...] = dot(weighted, c[:, own], 0, 0)
    grad_c[...] = dot(weighted, b[:, own], 1, 0)
    gains = terms(jnp.broadcast_to(columns(gain[...]), (gain.shape[1], 128)), 3)
    for part, chunk in enumerate(chunks):
        spread = head_spread((wx[0], wx[1]), chunk)
        rows = dy[:, pl.ds(chunk * CHUNK, CHUNK)].astype(F32)
        skip = head_spread(gains, chunk)[0:1, :] * rows
        spread_out[:, pl.ds(part * CHUNK, CHUNK)] = spread
        grad_x[:, pl.ds(part * CHUNK, CHUNK)] = (
            spread * dot(scores, piece(dyw, chunk, starts), 0, 0) + skip
        )


def relay_kernel(*refs, turn, even_links, ranks, starts):
    out, refs = refs[-1], refs[:-1]
    count = len(starts)
    states, decays, got = refs[:count], refs[count : 2 * count], refs[2 * count :]
    forward, lag = heading(even_links, ranks)
    kind = jnp.where(forward, 0, 1)
    chunk = turn - lag
    state = shrink = None
    for start, state_ref, decay_ref in zip(starts, states, decays):
        place = jnp.clip(chunk - start, 0, state_ref.shape[0] - 1)
        if state is None:
            state, shrink = state_ref[place, kind], decay_ref[place]
        else:
            state = jnp.where(chunk >= start, state_ref[place, kind], state)
            shrink = jnp.where(chunk >= start, decay_ref[place], shrink)
    if got:
        state = got[0][...].astype(F32) * shrink + state
    out[...] = state.astype(BF16)


def chosen(candidates, source):
    value = jnp.zeros(candidates[0].shape, BF16)
    for place, candidate in enumerate(candidates):
        value = jnp.where(source == place, candidate[...], value)
    return value


def carried_kernel(*refs, chunk, per_group, last, ranks, start):
    rank = lax.axis_index("ctx")
    fwd_in = chosen(refs[: ranks - 1], rank - 1)
    back_in = chosen(refs[: ranks - 1], ranks - 2 - rank)
    refs = refs[ranks - 1 :]
    dyw, xw, b, decay, spread, part_x, part_b, part_c = refs[:8]
    group, inside = chunk // per_group, chunk % per_group
    grad_x, grad_b, grad_c = refs[-7 if last else -5 :][:3]
    x_out = refs[-4] if last else refs[-2]
    sems = refs[-1]
    place = chunk - start
    span = pl.ds(place * CHUNK, CHUNK)
    own = pl.ds(group * N, N)
    copies = []

    def send(source, target, place):
        copies.append(pltpu.make_async_copy(source, target, sems.at[place]))
        copies[-1].start()

    back = (back_in.astype(F32) * decay[place]).astype(BF16)
    part = pl.ds(inside * CHUNK, CHUNK)
    carried = spread[:, part] * dot(b[:, own], back, 1, 0)
    x_out[...] = (part_x[:, part] + carried).astype(BF16)
    send(x_out, grad_x.at[:, pl.ds(chunk * CHUNK, CHUNK)], 0)
    total_b = part_b[...] + dot(xw[:, span], back, 1, 1)
    if last:
        b_out, c_out = refs[-3:-1]
        b_out[...] = total_b.astype(BF16)
        send(b_out, grad_b.at[:, own], 1)
    else:
        grad_b[...] = total_b
    total_c = part_c[...] + dot(dyw[:, span], fwd_in, 1, 1)
    if last:
        c_out[...] = total_c.astype(BF16)
        send(c_out, grad_c.at[:, own], 2)
    else:
        grad_c[...] = total_c
    for copy in copies:
        copy.wait()


def cost(flops, bytes_accessed):
    return pl.CostEstimate(flops=flops, bytes_accessed=bytes_accessed, transcendentals=0)


def on_device(grad_out, saved_x, saved_b, saved_c, step_size, decay_rate, skip_gain):
    tokens, row_width = grad_out.shape
    head_count = step_size.shape[1]
    groups = saved_b.shape[1] // N
    chunks = row_width // CHUNK
    per_group = chunks // groups
    group_width = row_width // groups
    ranks = lax.axis_size("ctx")
    gain_row = skip_gain.reshape(1, head_count)
    stay = partial(pltpu.with_memory_space_constraint, memory_space=pltpu.HBM)
    sources = [stay(array) for array in (grad_out, saved_x, saved_b, saved_c)]
    starts = [start for start in (0, 2) if start < chunks]
    stops = starts[1:] + [chunks]

    def local_states(first, last, inputs, in_spec, extra_shapes, extra_scratch):
        wide = (last - first) * CHUNK
        out_shape = [
            pltpu.VMEM((tokens, wide), BF16),
            pltpu.VMEM((tokens, wide), BF16),
            pltpu.VMEM((last - first, 2, N, CHUNK), F32),
            pltpu.VMEM((last - first, 1, CHUNK), F32),
        ] + extra_shapes
        tall = ((last - 1) // per_group - first // per_group + 1) * N
        return pl.pallas_call(
            partial(local_kernel, first=first, last=last, per_group=per_group),
            in_specs=[in_spec] * 2 + [ANYWHERE] * 4,
            out_specs=[IN_VMEM] * len(out_shape),
            out_shape=out_shape,
            scratch_shapes=extra_scratch
            + [
                pltpu.VMEM((tokens, wide), BF16),
                pltpu.VMEM((tokens, wide), BF16),
                pltpu.VMEM((tokens, tall), BF16),
                pltpu.VMEM((tokens, tall), BF16),
                pltpu.SemaphoreType.DMA((6,)),
            ],
            compiler_params=PARAMS,
            cost_estimate=cost(4 * tokens * wide * (N + 512), 6 * tokens * wide),
            name=f"states_{first}",
        )(*inputs)

    small_scratch = [
        pltpu.VMEM((head_count, tokens), BF16),
        pltpu.VMEM((1, head_count), F32),
    ]
    step_rows, rate_row = step_size.T, decay_rate.reshape(1, head_count)
    first_send = pl.pallas_call(
        partial(first_kernel, ranks=ranks),
        in_specs=[ANYWHERE] * 6,
        out_specs=IN_VMEM,
        out_shape=pltpu.VMEM((N, CHUNK), BF16),
        scratch_shapes=small_scratch
        + [
            pltpu.VMEM((tokens, CHUNK), BF16),
            pltpu.VMEM((tokens, N), BF16),
            pltpu.SemaphoreType.DMA((4,)),
        ],
        compiler_params=PARAMS,
        cost_estimate=cost(2 * tokens * CHUNK * (N + 256), 4 * tokens * CHUNK),
        name="first_state",
    )(stay(step_rows), stay(rate_row), *sources)
    rate_row, _ = lax.optimization_barrier((rate_row, first_send))
    *head, wd, wx = local_states(
        0,
        stops[0],
        [stay(step_rows), stay(rate_row)] + sources,
        ANYWHERE,
        [pltpu.VMEM((2, head_count, tokens), BF16)] * 2,
        small_scratch,
    )
    pieces = [head]

    def more_states(wd):
        place = len(pieces)
        pieces.append(
            local_states(
                starts[place], stops[place], [wd, wx] + sources, IN_VMEM, [], []
            )
        )

    def within(group, wx):
        return pl.pallas_call(
            partial(within_kernel, group=group, per_group=per_group, starts=starts),
            in_specs=[IN_VMEM] * (2 * len(starts) + 5),
            out_specs=[IN_VMEM] * 4,
            out_shape=[
                pltpu.VMEM((tokens, group_width), F32),
                pltpu.VMEM((tokens, N), F32),
                pltpu.VMEM((tokens, N), F32),
                pltpu.VMEM((tokens, group_width), F32),
            ],
            compiler_params=PARAMS,
            cost_estimate=cost(
                4 * tokens * tokens * (group_width + 2 * N), 10 * tokens * group_width
            ),
            name=f"within_{group}",
        )(
            *[piece[0] for piece in pieces],
            *[piece[1] for piece in pieces],
            saved_b,
            saved_c,
            grad_out,
            wx,
            gain_row,
        )

    def relay(turn, even_links, got):
        top = turn if even_links else turn - 1
        count = sum(start <= top for start in starts)
        got = [] if got is None else [got]
        return pl.pallas_call(
            partial(
                relay_kernel,
                turn=turn,
                even_links=even_links,
                ranks=ranks,
                starts=starts[:count],
            ),
            in_specs=[IN_VMEM] * (2 * count + len(got)),
            out_specs=IN_VMEM,
            out_shape=pltpu.VMEM((N, CHUNK), BF16),
            compiler_params=RELAY_PARAMS,
            cost_estimate=cost(4 * N * CHUNK, 8 * N * CHUNK),
            name=f"relay_{turn}",
        )(
            *[piece[2] for piece in pieces[:count]],
            *[piece[3] for piece in pieces[:count]],
            *got,
        )

    def carried(chunk, candidates, spread, part_x, part_b, part_c, grads):
        place = max(i for i, start in enumerate(starts) if start <= chunk)
        own = pieces[place]
        last = chunk % per_group == per_group - 1
        out_shape = [jax.ShapeDtypeStruct((tokens, row_width), BF16)]
        out_specs = [ANYWHERE]
        scratch = [pltpu.VMEM((tokens, CHUNK), BF16)]
        if last:
            out_shape += [jax.ShapeDtypeStruct((tokens, groups * N), BF16)] * 2
            out_specs += [ANYWHERE] * 2
            scratch += [pltpu.VMEM((tokens, N), BF16)] * 2
        else:
            out_shape += [pltpu.VMEM((tokens, N), F32)] * 2
            out_specs += [IN_VMEM] * 2
        inputs = [*candidates, own[0], own[1], saved_b, own[3], spread, part_x, part_b, part_c]
        aliases = {}
        if grads[0] is not None:
            aliases[len(inputs)] = 0
            inputs.append(grads[0])
        if last and grads[1] is not None:
            for slot in (1, 2):
                aliases[len(inputs)] = slot
                inputs.append(grads[slot])
        results = pl.pallas_call(
            partial(
                carried_kernel,
                chunk=chunk,
                per_group=per_group,
                last=last,
                ranks=ranks,
                start=starts[place],
            ),
            in_specs=[IN_VMEM] * (ranks + 7) + [ANYWHERE] * len(aliases),
            out_specs=out_specs,
            out_shape=out_shape,
            scratch_shapes=scratch + [pltpu.SemaphoreType.DMA((3,))],
            input_output_aliases=aliases,
            compiler_params=PARAMS,
            cost_estimate=cost(6 * tokens * CHUNK * N, 14 * tokens * CHUNK),
            name=f"carried_{chunk}",
        )(*inputs)
        if last:
            return None, list(results)
        return results[1:], [results[0]] + list(grads[1:])

    def links(turn, even_links):
        pairs = []
        for low in range(0 if even_links else 1, ranks - 1, 2):
            if 0 <= turn - low < chunks:
                pairs.append((low, low + 1))
            if 0 <= turn - (ranks - 2 - low) < chunks:
                pairs.append((low + 1, low))
        return pairs

    turns = chunks + ranks - 2
    order = []
    for base in range(turns):
        for turn in (base, base + 1):
            even_links = base % 2 == 0
            if turn < turns and links(turn, even_links):
                order.append((turn, even_links))
    got, parts = {}, {}
    sums, grads = None, [None, None, None]
    groups_left, chunks_left = list(range(groups)), list(range(chunks))

    def carry():
        nonlocal sums, grads
        chunk = chunks_left.pop(0)
        candidates = [got[chunk + hop, hop % 2 == 0] for hop in range(ranks - 1)]
        part_x, part_b, part_c, spread = parts[chunk // per_group]
        if chunk % per_group > 0:
            part_b, part_c = sums
        sums, grads = carried(chunk, candidates, spread, part_x, part_b, part_c, grads)

    for position, (turn, even_links) in enumerate(order):
        before = got.get((turn - 1, not even_links))
        send = first_send if position == 0 else relay(turn, even_links, before)
        key = (turn, even_links)
        got[key] = lax.ppermute(send, "ctx", links(turn, even_links))
        ready = order[: position - 1]
        following = order[position - 1] if position else None
        if position == 1:
            while len(pieces) < len(starts):
                more_states(lax.optimization_barrier((wd, send))[0])
                pieces[-1], got[following] = lax.optimization_barrier(
                    (pieces[-1], got[following])
                )
        elif position % 2 == 0 and position > 0:
            if groups_left and position >= min(4, len(order) - 2):
                held = lax.optimization_barrier((wx, before))[0]
                while groups_left:
                    group = groups_left.pop(0)
                    parts[group] = within(group, held)
                    parts[group], got[following] = lax.optimization_barrier(
                        (parts[group], got[following])
                    )
            elif not groups_left and (chunks_left[0] + ranks - 2, True) in ready:
                carry()
                grads[0], got[following] = lax.optimization_barrier((grads[0], got[following]))
    while groups_left:
        group = groups_left.pop(0)
        parts[group] = within(group, wx)
    while chunks_left:
        carry()
    return tuple(grads)


def solution(mesh):
    rows_cols = P(("groups", "ctx"), ("dp", "inner"))
    return jax.shard_map(
        on_device,
        mesh=mesh,
        in_specs=(rows_cols,) * 5 + (P(("dp", "inner")),) * 2,
        out_specs=(rows_cols,) * 3,
        check_vma=False,
    )
```

```python
from functools import partial

import jax
import jax.numpy as jnp
from jax import lax
from jax.experimental import pallas as pl
from jax.experimental.pallas import tpu as pltpu
from jax.sharding import PartitionSpec as P

P_SIZE = 64
N = 256
CHUNK = 512
CHUNK_HEADS = CHUNK // P_SIZE
F32 = jnp.float32
BF16 = jnp.bfloat16
PARAMS = pltpu.CompilerParams(vmem_limit_bytes=16 * 1024 * 1024)
RELAY_PARAMS = pltpu.CompilerParams(vmem_limit_bytes=4 * 1024 * 1024)
ANYWHERE = pl.BlockSpec(memory_space=pl.ANY)
IN_VMEM = pl.BlockSpec(memory_space=pltpu.VMEM)


def dot(left, right, left_dim, right_dim):
    return lax.dot_general(
        left, right, (((left_dim,), (right_dim,)), ((), ())), preferred_element_type=F32
    )


def terms(value, count):
    parts = []
    for _ in range(count):
        part = value.astype(BF16)
        parts.append(part)
        value = value - part.astype(F32)
    return parts


def head_spread(parts, chunk):
    head_count = parts[0].shape[0]
    shape = (len(parts) * head_count, CHUNK)
    head = lax.rem(lax.broadcasted_iota(jnp.int32, shape, 0), head_count)
    cols = lax.broadcasted_iota(jnp.int32, shape, 1)
    pick = (head == chunk * CHUNK_HEADS + cols // P_SIZE).astype(F32).astype(BF16)
    return dot(jnp.concatenate(parts, axis=0), pick, 0, 0)


def lower_mask(tokens):
    rows = lax.broadcasted_iota(jnp.int32, (tokens, tokens), 0)
    cols = lax.broadcasted_iota(jnp.int32, (tokens, tokens), 1)
    return rows >= cols


def columns(row):
    size = row.shape[1]
    rows = lax.broadcasted_iota(jnp.int32, (size, size), 0)
    cols = lax.broadcasted_iota(jnp.int32, (size, size), 1)
    return jnp.sum(jnp.where(rows == cols, row, 0.0), axis=1, keepdims=True)


def heading(even_links, ranks):
    rank = lax.axis_index("ctx")
    forward = (lax.rem(rank, 2) == 0) == even_links
    return forward, jnp.where(forward, rank, ranks - 1 - rank)


def upper_ones(tokens):
    rows = lax.broadcasted_iota(jnp.int32, (tokens, tokens), 0)
    cols = lax.broadcasted_iota(jnp.int32, (tokens, tokens), 1)
    return (rows <= cols).astype(F32).astype(BF16)


def first_kernel(step_hbm, rate_hbm, dy, x, b, c, send, step, rate, rows_in, group_in, sems, *, ranks):
    rank = lax.axis_index("ctx")

    def fetch(source, target, place):
        if source.shape != target.shape:
            source = source.at[:, pl.ds(0, target.shape[1])]
        copy = pltpu.make_async_copy(source, target, sems.at[place])
        copy.start()
        return copy

    def state(wide, narrow, weigh):
        copies = [
            fetch(step_hbm, step, 0),
            fetch(rate_hbm, rate, 1),
            fetch(wide, rows_in, 2),
            fetch(narrow, group_in, 3),
        ]
        upper = upper_ones(step.shape[1])
        copies[0].wait()
        copies[1].wait()
        cum = dot(step[...], upper, 1, 0) * columns(rate[...])
        spread = head_spread(terms(weigh(cum), 2), 0)
        copies[2].wait()
        rows = (spread * rows_in[...].astype(F32)).astype(BF16)
        copies[3].wait()
        send[...] = dot(group_in[...], rows, 0, 0).astype(BF16)

    @pl.when(rank == 0)
    def _():
        state(x, b, lambda cum: jnp.exp(cum[:, -1:] - cum) * step[...].astype(F32))

    @pl.when(rank == ranks - 1)
    def _():
        state(dy, c, jnp.exp)


def local_kernel(*refs, first, last, per_group):
    if first == 0:
        step_hbm, rate_hbm, dy, x, b, c = refs[:6]
        dyw, xw, states, decay, wd, wx = refs[6:12]
        step, rate, dy_in, x_in, b_in, c_in, sems = refs[12:]
    else:
        wd, wx, dy, x, b, c = refs[:6]
        dyw, xw, states, decay = refs[6:10]
        dy_in, x_in, b_in, c_in, sems = refs[10:]
    tokens = dy_in.shape[0]
    low_group = first // per_group

    def fetch(source, target, place):
        copy = pltpu.make_async_copy(source, target, sems.at[place])
        copy.start()
        return copy

    def part(source, target, low, place):
        return fetch(source.at[:, pl.ds(low, target.shape[1])], target, place)

    if first == 0:
        small = [fetch(step_hbm, step, 4), fetch(rate_hbm, rate, 5)]
    copies = [
        part(dy, dy_in, first * CHUNK, 0),
        part(c, c_in, low_group * N, 1),
        part(x, x_in, first * CHUNK, 2),
        part(b, b_in, low_group * N, 3),
    ]
    if first == 0:
        upper = upper_ones(tokens)
        for copy in small:
            copy.wait()
        cum = dot(step[...], upper, 1, 0) * columns(rate[...])
        wd[0], wd[1] = terms(jnp.exp(cum), 2)
        wx[0], wx[1] = terms(jnp.exp(-cum) * step[...].astype(F32), 2)
    for copy in copies:
        copy.wait()
    for chunk in range(first, last):
        place = chunk - first
        span = pl.ds(place * CHUNK, CHUNK)
        group = pl.ds((chunk // per_group - low_group) * N, N)
        spread = head_spread((wd[0], wd[1]), chunk)
        end = spread[tokens - 1 : tokens, :]
        decay[place] = end
        dyw[:, span] = (spread * dy_in[:, span].astype(F32)).astype(BF16)
        spread = head_spread((wx[0], wx[1]), chunk)
        xw[:, span] = (spread * x_in[:, span].astype(F32)).astype(BF16)
        states[place, 1] = dot(c_in[:, group], dyw[:, span], 0, 0)
        states[place, 0] = dot(b_in[:, group], xw[:, span], 0, 0) * end


def piece(refs, chunk, starts):
    place = max(i for i, start in enumerate(starts) if start <= chunk)
    return refs[place][:, pl.ds((chunk - starts[place]) * CHUNK, CHUNK)]


def within_kernel(*refs, group, per_group, starts):
    count = len(starts)
    dyw, xw, refs = refs[:count], refs[count : 2 * count], refs[2 * count :]
    b, c, dy, wx, gain, grad_x, grad_b, grad_c, spread_out = refs
    lower = lower_mask(b.shape[0])
    own = pl.ds(group * N, N)
    chunks = range(group * per_group, (group + 1) * per_group)
    scores = jnp.where(lower, dot(c[:, own], b[:, own], 1, 1), 0.0).astype(BF16)
    weighted = sum(
        dot(piece(dyw, chunk, starts), piece(xw, chunk, starts), 1, 1) for chunk in chunks
    )
    weighted = jnp.where(lower, weighted, 0.0).astype(BF16)
    grad_b[...] = dot(weighted, c[:, own], 0, 0)
    grad_c[...] = dot(weighted, b[:, own], 1, 0)
    gains = terms(jnp.broadcast_to(columns(gain[...]), (gain.shape[1], 128)), 3)
    for part, chunk in enumerate(chunks):
        spread = head_spread((wx[0], wx[1]), chunk)
        rows = dy[:, pl.ds(chunk * CHUNK, CHUNK)].astype(F32)
        skip = head_spread(gains, chunk)[0:1, :] * rows
        spread_out[:, pl.ds(part * CHUNK, CHUNK)] = spread
        grad_x[:, pl.ds(part * CHUNK, CHUNK)] = (
            spread * dot(scores, piece(dyw, chunk, starts), 0, 0) + skip
        )


def relay_kernel(*refs, turn, even_links, ranks, starts):
    out, refs = refs[-1], refs[:-1]
    count = len(starts)
    states, decays, got = refs[:count], refs[count : 2 * count], refs[2 * count :]
    forward, lag = heading(even_links, ranks)
    kind = jnp.where(forward, 0, 1)
    chunk = turn - lag
    state = shrink = None
    for start, state_ref, decay_ref in zip(starts, states, decays):
        place = jnp.clip(chunk - start, 0, state_ref.shape[0] - 1)
        if state is None:
            state, shrink = state_ref[place, kind], decay_ref[place]
        else:
            state = jnp.where(chunk >= start, state_ref[place, kind], state)
            shrink = jnp.where(chunk >= start, decay_ref[place], shrink)
    if got:
        state = got[0][...].astype(F32) * shrink + state
    out[...] = state.astype(BF16)


def chosen(candidates, source):
    value = jnp.zeros(candidates[0].shape, BF16)
    for place, candidate in enumerate(candidates):
        value = jnp.where(source == place, candidate[...], value)
    return value


def carried_kernel(*refs, chunk, per_group, last, ranks, start):
    rank = lax.axis_index("ctx")
    fwd_in = chosen(refs[: ranks - 1], rank - 1)
    back_in = chosen(refs[: ranks - 1], ranks - 2 - rank)
    refs = refs[ranks - 1 :]
    dyw, xw, b, decay, spread, part_x, part_b, part_c = refs[:8]
    group, inside = chunk // per_group, chunk % per_group
    grad_x, grad_b, grad_c = refs[-7 if last else -5 :][:3]
    x_out = refs[-4] if last else refs[-2]
    sems = refs[-1]
    place = chunk - start
    span = pl.ds(place * CHUNK, CHUNK)
    own = pl.ds(group * N, N)
    copies = []

    def send(source, target, place):
        copies.append(pltpu.make_async_copy(source, target, sems.at[place]))
        copies[-1].start()

    back = (back_in.astype(F32) * decay[place]).astype(BF16)
    part = pl.ds(inside * CHUNK, CHUNK)
    half = b.shape[0] // 2
    for low in (0, half):
        rows = pl.ds(low, half)
        slot = 3 * (low > 0)
        carried = spread[rows, part] * dot(b[rows, own], back, 1, 0)
        x_out[rows] = (part_x[rows, part] + carried).astype(BF16)
        send(x_out.at[rows], grad_x.at[rows, pl.ds(chunk * CHUNK, CHUNK)], slot)
        total_b = part_b[rows] + dot(xw[rows, span], back, 1, 1)
        total_c = part_c[rows] + dot(dyw[rows, span], fwd_in, 1, 1)
        if last:
            b_out, c_out = refs[-3:-1]
            b_out[rows] = total_b.astype(BF16)
            send(b_out.at[rows], grad_b.at[rows, own], slot + 1)
            c_out[rows] = total_c.astype(BF16)
            send(c_out.at[rows], grad_c.at[rows, own], slot + 2)
        else:
            grad_b[rows] = total_b
            grad_c[rows] = total_c
    for copy in copies:
        copy.wait()


def cost(flops, bytes_accessed):
    return pl.CostEstimate(flops=flops, bytes_accessed=bytes_accessed, transcendentals=0)


def on_device(grad_out, saved_x, saved_b, saved_c, step_size, decay_rate, skip_gain):
    tokens, row_width = grad_out.shape
    head_count = step_size.shape[1]
    groups = saved_b.shape[1] // N
    chunks = row_width // CHUNK
    per_group = chunks // groups
    group_width = row_width // groups
    ranks = lax.axis_size("ctx")
    gain_row = skip_gain.reshape(1, head_count)
    stay = partial(pltpu.with_memory_space_constraint, memory_space=pltpu.HBM)
    sources = [stay(array) for array in (grad_out, saved_x, saved_b, saved_c)]
    starts = [start for start in (0, 2) if start < chunks]
    stops = starts[1:] + [chunks]

    def local_states(first, last, inputs, in_spec, extra_shapes, extra_scratch):
        wide = (last - first) * CHUNK
        out_shape = [
            pltpu.VMEM((tokens, wide), BF16),
            pltpu.VMEM((tokens, wide), BF16),
            pltpu.VMEM((last - first, 2, N, CHUNK), F32),
            pltpu.VMEM((last - first, 1, CHUNK), F32),
        ] + extra_shapes
        tall = ((last - 1) // per_group - first // per_group + 1) * N
        return pl.pallas_call(
            partial(local_kernel, first=first, last=last, per_group=per_group),
            in_specs=[in_spec] * 2 + [ANYWHERE] * 4,
            out_specs=[IN_VMEM] * len(out_shape),
            out_shape=out_shape,
            scratch_shapes=extra_scratch
            + [
                pltpu.VMEM((tokens, wide), BF16),
                pltpu.VMEM((tokens, wide), BF16),
                pltpu.VMEM((tokens, tall), BF16),
                pltpu.VMEM((tokens, tall), BF16),
                pltpu.SemaphoreType.DMA((6,)),
            ],
            compiler_params=PARAMS,
            cost_estimate=cost(4 * tokens * wide * (N + 512), 6 * tokens * wide),
            name=f"states_{first}",
        )(*inputs)

    small_scratch = [
        pltpu.VMEM((head_count, tokens), BF16),
        pltpu.VMEM((1, head_count), F32),
    ]
    step_rows, rate_row = step_size.T, decay_rate.reshape(1, head_count)
    first_send = pl.pallas_call(
        partial(first_kernel, ranks=ranks),
        in_specs=[ANYWHERE] * 6,
        out_specs=IN_VMEM,
        out_shape=pltpu.VMEM((N, CHUNK), BF16),
        scratch_shapes=small_scratch
        + [
            pltpu.VMEM((tokens, CHUNK), BF16),
            pltpu.VMEM((tokens, N), BF16),
            pltpu.SemaphoreType.DMA((4,)),
        ],
        compiler_params=PARAMS,
        cost_estimate=cost(2 * tokens * CHUNK * (N + 256), 4 * tokens * CHUNK),
        name="first_state",
    )(stay(step_rows), stay(rate_row), *sources)
    rate_row, _ = lax.optimization_barrier((rate_row, first_send))
    *head, wd, wx = local_states(
        0,
        stops[0],
        [stay(step_rows), stay(rate_row)] + sources,
        ANYWHERE,
        [pltpu.VMEM((2, head_count, tokens), BF16)] * 2,
        small_scratch,
    )
    pieces = [head]

    def more_states(wd):
        place = len(pieces)
        pieces.append(
            local_states(
                starts[place], stops[place], [wd, wx] + sources, IN_VMEM, [], []
            )
        )

    def within(group, wx):
        return pl.pallas_call(
            partial(within_kernel, group=group, per_group=per_group, starts=starts),
            in_specs=[IN_VMEM] * (2 * len(starts) + 5),
            out_specs=[IN_VMEM] * 4,
            out_shape=[
                pltpu.VMEM((tokens, group_width), F32),
                pltpu.VMEM((tokens, N), F32),
                pltpu.VMEM((tokens, N), F32),
                pltpu.VMEM((tokens, group_width), F32),
            ],
            compiler_params=PARAMS,
            cost_estimate=cost(
                4 * tokens * tokens * (group_width + 2 * N), 10 * tokens * group_width
            ),
            name=f"within_{group}",
        )(
            *[piece[0] for piece in pieces],
            *[piece[1] for piece in pieces],
            saved_b,
            saved_c,
            grad_out,
            wx,
            gain_row,
        )

    def relay(turn, even_links, got):
        top = turn if even_links else turn - 1
        count = sum(start <= top for start in starts)
        got = [] if got is None else [got]
        return pl.pallas_call(
            partial(
                relay_kernel,
                turn=turn,
                even_links=even_links,
                ranks=ranks,
                starts=starts[:count],
            ),
            in_specs=[IN_VMEM] * (2 * count + len(got)),
            out_specs=IN_VMEM,
            out_shape=pltpu.VMEM((N, CHUNK), BF16),
            compiler_params=RELAY_PARAMS,
            cost_estimate=cost(4 * N * CHUNK, 8 * N * CHUNK),
            name=f"relay_{turn}",
        )(
            *[piece[2] for piece in pieces[:count]],
            *[piece[3] for piece in pieces[:count]],
            *got,
        )

    def carried(chunk, candidates, spread, part_x, part_b, part_c, grads):
        place = max(i for i, start in enumerate(starts) if start <= chunk)
        own = pieces[place]
        last = chunk % per_group == per_group - 1
        out_shape = [jax.ShapeDtypeStruct((tokens, row_width), BF16)]
        out_specs = [ANYWHERE]
        scratch = [pltpu.VMEM((tokens, CHUNK), BF16)]
        if last:
            out_shape += [jax.ShapeDtypeStruct((tokens, groups * N), BF16)] * 2
            out_specs += [ANYWHERE] * 2
            scratch += [pltpu.VMEM((tokens, N), BF16)] * 2
        else:
            out_shape += [pltpu.VMEM((tokens, N), F32)] * 2
            out_specs += [IN_VMEM] * 2
        inputs = [*candidates, own[0], own[1], saved_b, own[3], spread, part_x, part_b, part_c]
        aliases = {}
        if grads[0] is not None:
            aliases[len(inputs)] = 0
            inputs.append(grads[0])
        if last and grads[1] is not None:
            for slot in (1, 2):
                aliases[len(inputs)] = slot
                inputs.append(grads[slot])
        results = pl.pallas_call(
            partial(
                carried_kernel,
                chunk=chunk,
                per_group=per_group,
                last=last,
                ranks=ranks,
                start=starts[place],
            ),
            in_specs=[IN_VMEM] * (ranks + 7) + [ANYWHERE] * len(aliases),
            out_specs=out_specs,
            out_shape=out_shape,
            scratch_shapes=scratch + [pltpu.SemaphoreType.DMA((6,))],
            input_output_aliases=aliases,
            compiler_params=PARAMS,
            cost_estimate=cost(6 * tokens * CHUNK * N, 14 * tokens * CHUNK),
            name=f"carried_{chunk}",
        )(*inputs)
        if last:
            return None, list(results)
        return results[1:], [results[0]] + list(grads[1:])

    def links(turn, even_links):
        pairs = []
        for low in range(0 if even_links else 1, ranks - 1, 2):
            if 0 <= turn - low < chunks:
                pairs.append((low, low + 1))
            if 0 <= turn - (ranks - 2 - low) < chunks:
                pairs.append((low + 1, low))
        return pairs

    turns = chunks + ranks - 2
    order = []
    for base in range(turns):
        for turn in (base, base + 1):
            even_links = base % 2 == 0
            if turn < turns and links(turn, even_links):
                order.append((turn, even_links))
    got, parts = {}, {}
    sums, grads = None, [None, None, None]
    groups_left, chunks_left = list(range(groups)), list(range(chunks))

    def carry():
        nonlocal sums, grads
        chunk = chunks_left.pop(0)
        candidates = [got[chunk + hop, hop % 2 == 0] for hop in range(ranks - 1)]
        part_x, part_b, part_c, spread = parts[chunk // per_group]
        if chunk % per_group > 0:
            part_b, part_c = sums
        sums, grads = carried(chunk, candidates, spread, part_x, part_b, part_c, grads)

    for position, (turn, even_links) in enumerate(order):
        before = got.get((turn - 1, not even_links))
        send = first_send if position == 0 else relay(turn, even_links, before)
        key = (turn, even_links)
        got[key] = lax.ppermute(send, "ctx", links(turn, even_links))
        ready = order[: position - 1]
        following = order[position - 1] if position else None
        if position == 1:
            while len(pieces) < len(starts):
                more_states(lax.optimization_barrier((wd, send))[0])
                pieces[-1], got[following] = lax.optimization_barrier(
                    (pieces[-1], got[following])
                )
        elif position % 2 == 0 and position > 0:
            if groups_left and position >= min(4, len(order) - 2):
                held = lax.optimization_barrier((wx, before))[0]
                while groups_left:
                    group = groups_left.pop(0)
                    parts[group] = within(group, held)
                    parts[group], got[following] = lax.optimization_barrier(
                        (parts[group], got[following])
                    )
            elif not groups_left and (chunks_left[0] + ranks - 2, True) in ready:
                carry()
                grads[0], got[following] = lax.optimization_barrier((grads[0], got[following]))
    while groups_left:
        group = groups_left.pop(0)
        parts[group] = within(group, wx)
    while chunks_left:
        carry()
    return tuple(grads)


def solution(mesh):
    rows_cols = P(("groups", "ctx"), ("dp", "inner"))
    return jax.shard_map(
        on_device,
        mesh=mesh,
        in_specs=(rows_cols,) * 5 + (P(("dp", "inner")),) * 2,
        out_specs=(rows_cols,) * 3,
        check_vma=False,
    )
```

```python
from functools import partial

import jax
import jax.numpy as jnp
from jax import lax
from jax.experimental import pallas as pl
from jax.experimental.pallas import tpu as pltpu
from jax.sharding import PartitionSpec as P

P_SIZE = 64
N = 256
CHUNK = 512
CHUNK_HEADS = CHUNK // P_SIZE
F32 = jnp.float32
BF16 = jnp.bfloat16
PARAMS = pltpu.CompilerParams(vmem_limit_bytes=16 * 1024 * 1024)
RELAY_PARAMS = pltpu.CompilerParams(vmem_limit_bytes=4 * 1024 * 1024)
ANYWHERE = pl.BlockSpec(memory_space=pl.ANY)
IN_VMEM = pl.BlockSpec(memory_space=pltpu.VMEM)


def dot(left, right, left_dim, right_dim):
    return lax.dot_general(
        left, right, (((left_dim,), (right_dim,)), ((), ())), preferred_element_type=F32
    )


def terms(value, count):
    parts = []
    for _ in range(count):
        part = value.astype(BF16)
        parts.append(part)
        value = value - part.astype(F32)
    return parts


def head_spread(parts, chunk):
    head_count = parts[0].shape[0]
    shape = (len(parts) * head_count, CHUNK)
    head = lax.rem(lax.broadcasted_iota(jnp.int32, shape, 0), head_count)
    cols = lax.broadcasted_iota(jnp.int32, shape, 1)
    pick = (head == chunk * CHUNK_HEADS + cols // P_SIZE).astype(F32).astype(BF16)
    return dot(jnp.concatenate(parts, axis=0), pick, 0, 0)


def lower_mask(tokens):
    rows = lax.broadcasted_iota(jnp.int32, (tokens, tokens), 0)
    cols = lax.broadcasted_iota(jnp.int32, (tokens, tokens), 1)
    return rows >= cols


def columns(row):
    size = row.shape[1]
    rows = lax.broadcasted_iota(jnp.int32, (size, size), 0)
    cols = lax.broadcasted_iota(jnp.int32, (size, size), 1)
    return jnp.sum(jnp.where(rows == cols, row, 0.0), axis=1, keepdims=True)


def heading(even_links, ranks):
    rank = lax.axis_index("ctx")
    forward = (lax.rem(rank, 2) == 0) == even_links
    return forward, jnp.where(forward, rank, ranks - 1 - rank)


def upper_ones(tokens):
    rows = lax.broadcasted_iota(jnp.int32, (tokens, tokens), 0)
    cols = lax.broadcasted_iota(jnp.int32, (tokens, tokens), 1)
    return (rows <= cols).astype(F32).astype(BF16)


def first_kernel(step_hbm, rate_hbm, dy, x, b, c, send, step, rate, rows_in, group_in, sems, *, ranks):
    rank = lax.axis_index("ctx")

    def fetch(source, target, place):
        if source.shape != target.shape:
            source = source.at[:, pl.ds(0, target.shape[1])]
        copy = pltpu.make_async_copy(source, target, sems.at[place])
        copy.start()
        return copy

    def state(wide, narrow, weigh):
        copies = [
            fetch(step_hbm, step, 0),
            fetch(rate_hbm, rate, 1),
            fetch(wide, rows_in, 2),
            fetch(narrow, group_in, 3),
        ]
        upper = upper_ones(step.shape[1])
        copies[0].wait()
        copies[1].wait()
        cum = dot(step[...], upper, 1, 0) * columns(rate[...])
        spread = head_spread(terms(weigh(cum), 2), 0)
        copies[2].wait()
        rows = (spread * rows_in[...].astype(F32)).astype(BF16)
        copies[3].wait()
        send[...] = dot(group_in[...], rows, 0, 0).astype(BF16)

    @pl.when(rank == 0)
    def _():
        state(x, b, lambda cum: jnp.exp(cum[:, -1:] - cum) * step[...].astype(F32))

    @pl.when(rank == ranks - 1)
    def _():
        state(dy, c, jnp.exp)


def local_kernel(*refs, first, last, per_group):
    if first == 0:
        step_hbm, rate_hbm, dy, x, b, c = refs[:6]
        dyw, xw, states, decay, wd, wx = refs[6:12]
        step, rate, dy_in, x_in, b_in, c_in, sems = refs[12:]
    else:
        wd, wx, dy, x, b, c = refs[:6]
        dyw, xw, states, decay = refs[6:10]
        dy_in, x_in, b_in, c_in, sems = refs[10:]
    tokens = dy_in.shape[0]
    low_group = first // per_group

    def fetch(source, target, place):
        copy = pltpu.make_async_copy(source, target, sems.at[place])
        copy.start()
        return copy

    def part(source, target, low, place):
        return fetch(source.at[:, pl.ds(low, target.shape[1])], target, place)

    if first == 0:
        small = [fetch(step_hbm, step, 4), fetch(rate_hbm, rate, 5)]
    copies = [
        part(dy, dy_in, first * CHUNK, 0),
        part(c, c_in, low_group * N, 1),
        part(x, x_in, first * CHUNK, 2),
        part(b, b_in, low_group * N, 3),
    ]
    if first == 0:
        upper = upper_ones(tokens)
        for copy in small:
            copy.wait()
        cum = dot(step[...], upper, 1, 0) * columns(rate[...])
        wd[0], wd[1] = terms(jnp.exp(cum), 2)
        wx[0], wx[1] = terms(jnp.exp(-cum) * step[...].astype(F32), 2)
    for copy in copies:
        copy.wait()
    for chunk in range(first, last):
        place = chunk - first
        span = pl.ds(place * CHUNK, CHUNK)
        group = pl.ds((chunk // per_group - low_group) * N, N)
        spread = head_spread((wd[0], wd[1]), chunk)
        end = spread[tokens - 1 : tokens, :]
        decay[place] = end
        dyw[:, span] = (spread * dy_in[:, span].astype(F32)).astype(BF16)
        spread = head_spread((wx[0], wx[1]), chunk)
        xw[:, span] = (spread * x_in[:, span].astype(F32)).astype(BF16)
        states[place, 1] = dot(c_in[:, group], dyw[:, span], 0, 0)
        states[place, 0] = dot(b_in[:, group], xw[:, span], 0, 0) * end


def piece(refs, chunk, starts):
    place = max(i for i, start in enumerate(starts) if start <= chunk)
    return refs[place][:, pl.ds((chunk - starts[place]) * CHUNK, CHUNK)]


def within_kernel(*refs, group, per_group, starts):
    count = len(starts)
    dyw, xw, refs = refs[:count], refs[count : 2 * count], refs[2 * count :]
    b, c, dy, wx, gain, grad_x, grad_b, grad_c, spread_out = refs
    lower = lower_mask(b.shape[0])
    own = pl.ds(group * N, N)
    chunks = range(group * per_group, (group + 1) * per_group)
    half = b.shape[0] // 2
    b_own, c_own = b[:, own], c[:, own]

    def triangle(lefts, rights):
        pairs = list(zip(lefts, rights))
        top = sum(dot(left[:half], right[:half], 1, 1) for left, right in pairs)
        low = sum(dot(left[half:], right, 1, 1) for left, right in pairs)
        top = jnp.where(lower[:half, :half], top, 0.0).astype(BF16)
        return top, jnp.where(lower[half:], low, 0.0).astype(BF16)

    def turned(parts, right):
        top, low = parts
        upper_half = dot(top, right[:half], 0, 0) + dot(low[:, :half], right[half:], 0, 0)
        return upper_half, dot(low[:, half:], right[half:], 0, 0)

    scores = triangle([c_own], [b_own])
    weighted = triangle(
        [piece(dyw, chunk, starts) for chunk in chunks],
        [piece(xw, chunk, starts) for chunk in chunks],
    )
    grad_b[:half], grad_b[half:] = turned(weighted, c_own)
    grad_c[:half] = dot(weighted[0], b_own[:half], 1, 0)
    grad_c[half:] = dot(weighted[1], b_own, 1, 0)
    gains = terms(jnp.broadcast_to(columns(gain[...]), (gain.shape[1], 128)), 3)
    for part, chunk in enumerate(chunks):
        spread = head_spread((wx[0], wx[1]), chunk)
        rows = dy[:, pl.ds(chunk * CHUNK, CHUNK)].astype(F32)
        skip = head_spread(gains, chunk)[0:1, :] * rows
        spread_out[:, pl.ds(part * CHUNK, CHUNK)] = spread
        sums = turned(scores, piece(dyw, chunk, starts))
        for low, value in zip((0, half), sums):
            span = slice(low, low + half)
            grad_x[span, pl.ds(part * CHUNK, CHUNK)] = spread[span] * value + skip[span]


def relay_kernel(*refs, turn, even_links, ranks, starts):
    out, refs = refs[-1], refs[:-1]
    count = len(starts)
    states, decays, got = refs[:count], refs[count : 2 * count], refs[2 * count :]
    forward, lag = heading(even_links, ranks)
    kind = jnp.where(forward, 0, 1)
    chunk = turn - lag
    state = shrink = None
    for start, state_ref, decay_ref in zip(starts, states, decays):
        place = jnp.clip(chunk - start, 0, state_ref.shape[0] - 1)
        if state is None:
            state, shrink = state_ref[place, kind], decay_ref[place]
        else:
            state = jnp.where(chunk >= start, state_ref[place, kind], state)
            shrink = jnp.where(chunk >= start, decay_ref[place], shrink)
    if got:
        state = got[0][...].astype(F32) * shrink + state
    out[...] = state.astype(BF16)


def chosen(candidates, source):
    value = jnp.zeros(candidates[0].shape, BF16)
    for place, candidate in enumerate(candidates):
        value = jnp.where(source == place, candidate[...], value)
    return value


def carried_kernel(*refs, chunk, per_group, last, ranks, start):
    rank = lax.axis_index("ctx")
    fwd_in = chosen(refs[: ranks - 1], rank - 1)
    back_in = chosen(refs[: ranks - 1], ranks - 2 - rank)
    refs = refs[ranks - 1 :]
    dyw, xw, b, decay, spread, part_x, part_b, part_c = refs[:8]
    group, inside = chunk // per_group, chunk % per_group
    grad_x, grad_b, grad_c = refs[-7 if last else -5 :][:3]
    x_out = refs[-4] if last else refs[-2]
    sems = refs[-1]
    place = chunk - start
    span = pl.ds(place * CHUNK, CHUNK)
    own = pl.ds(group * N, N)
    copies = []

    def send(source, target, place):
        copies.append(pltpu.make_async_copy(source, target, sems.at[place]))
        copies[-1].start()

    back = (back_in.astype(F32) * decay[place]).astype(BF16)
    part = pl.ds(inside * CHUNK, CHUNK)
    half = b.shape[0] // 2
    for low in (0, half):
        rows = pl.ds(low, half)
        slot = 3 * (low > 0)
        carried = spread[rows, part] * dot(b[rows, own], back, 1, 0)
        x_out[rows] = (part_x[rows, part] + carried).astype(BF16)
        send(x_out.at[rows], grad_x.at[rows, pl.ds(chunk * CHUNK, CHUNK)], slot)
        total_b = part_b[rows] + dot(xw[rows, span], back, 1, 1)
        total_c = part_c[rows] + dot(dyw[rows, span], fwd_in, 1, 1)
        if last:
            b_out, c_out = refs[-3:-1]
            b_out[rows] = total_b.astype(BF16)
            send(b_out.at[rows], grad_b.at[rows, own], slot + 1)
            c_out[rows] = total_c.astype(BF16)
            send(c_out.at[rows], grad_c.at[rows, own], slot + 2)
        else:
            grad_b[rows] = total_b
            grad_c[rows] = total_c
    for copy in copies:
        copy.wait()


def cost(flops, bytes_accessed):
    return pl.CostEstimate(flops=flops, bytes_accessed=bytes_accessed, transcendentals=0)


def on_device(grad_out, saved_x, saved_b, saved_c, step_size, decay_rate, skip_gain):
    tokens, row_width = grad_out.shape
    head_count = step_size.shape[1]
    groups = saved_b.shape[1] // N
    chunks = row_width // CHUNK
    per_group = chunks // groups
    group_width = row_width // groups
    ranks = lax.axis_size("ctx")
    gain_row = skip_gain.reshape(1, head_count)
    stay = partial(pltpu.with_memory_space_constraint, memory_space=pltpu.HBM)
    sources = [stay(array) for array in (grad_out, saved_x, saved_b, saved_c)]
    starts = [start for start in (0, 2) if start < chunks]
    stops = starts[1:] + [chunks]

    def local_states(first, last, inputs, in_spec, extra_shapes, extra_scratch):
        wide = (last - first) * CHUNK
        out_shape = [
            pltpu.VMEM((tokens, wide), BF16),
            pltpu.VMEM((tokens, wide), BF16),
            pltpu.VMEM((last - first, 2, N, CHUNK), F32),
            pltpu.VMEM((last - first, 1, CHUNK), F32),
        ] + extra_shapes
        tall = ((last - 1) // per_group - first // per_group + 1) * N
        return pl.pallas_call(
            partial(local_kernel, first=first, last=last, per_group=per_group),
            in_specs=[in_spec] * 2 + [ANYWHERE] * 4,
            out_specs=[IN_VMEM] * len(out_shape),
            out_shape=out_shape,
            scratch_shapes=extra_scratch
            + [
                pltpu.VMEM((tokens, wide), BF16),
                pltpu.VMEM((tokens, wide), BF16),
                pltpu.VMEM((tokens, tall), BF16),
                pltpu.VMEM((tokens, tall), BF16),
                pltpu.SemaphoreType.DMA((6,)),
            ],
            compiler_params=PARAMS,
            cost_estimate=cost(4 * tokens * wide * (N + 512), 6 * tokens * wide),
            name=f"states_{first}",
        )(*inputs)

    small_scratch = [
        pltpu.VMEM((head_count, tokens), BF16),
        pltpu.VMEM((1, head_count), F32),
    ]
    step_rows, rate_row = step_size.T, decay_rate.reshape(1, head_count)
    first_send = pl.pallas_call(
        partial(first_kernel, ranks=ranks),
        in_specs=[ANYWHERE] * 6,
        out_specs=IN_VMEM,
        out_shape=pltpu.VMEM((N, CHUNK), BF16),
        scratch_shapes=small_scratch
        + [
            pltpu.VMEM((tokens, CHUNK), BF16),
            pltpu.VMEM((tokens, N), BF16),
            pltpu.SemaphoreType.DMA((4,)),
        ],
        compiler_params=PARAMS,
        cost_estimate=cost(2 * tokens * CHUNK * (N + 256), 4 * tokens * CHUNK),
        name="first_state",
    )(stay(step_rows), stay(rate_row), *sources)
    rate_row, _ = lax.optimization_barrier((rate_row, first_send))
    *head, wd, wx = local_states(
        0,
        stops[0],
        [stay(step_rows), stay(rate_row)] + sources,
        ANYWHERE,
        [pltpu.VMEM((2, head_count, tokens), BF16)] * 2,
        small_scratch,
    )
    pieces = [head]

    def more_states(wd):
        place = len(pieces)
        pieces.append(
            local_states(
                starts[place], stops[place], [wd, wx] + sources, IN_VMEM, [], []
            )
        )

    def within(group, wx):
        return pl.pallas_call(
            partial(within_kernel, group=group, per_group=per_group, starts=starts),
            in_specs=[IN_VMEM] * (2 * len(starts) + 5),
            out_specs=[IN_VMEM] * 4,
            out_shape=[
                pltpu.VMEM((tokens, group_width), F32),
                pltpu.VMEM((tokens, N), F32),
                pltpu.VMEM((tokens, N), F32),
                pltpu.VMEM((tokens, group_width), F32),
            ],
            compiler_params=PARAMS,
            cost_estimate=cost(
                4 * tokens * tokens * (group_width + 2 * N), 10 * tokens * group_width
            ),
            name=f"within_{group}",
        )(
            *[piece[0] for piece in pieces],
            *[piece[1] for piece in pieces],
            saved_b,
            saved_c,
            grad_out,
            wx,
            gain_row,
        )

    def relay(turn, even_links, got):
        top = turn if even_links else turn - 1
        count = sum(start <= top for start in starts)
        got = [] if got is None else [got]
        return pl.pallas_call(
            partial(
                relay_kernel,
                turn=turn,
                even_links=even_links,
                ranks=ranks,
                starts=starts[:count],
            ),
            in_specs=[IN_VMEM] * (2 * count + len(got)),
            out_specs=IN_VMEM,
            out_shape=pltpu.VMEM((N, CHUNK), BF16),
            compiler_params=RELAY_PARAMS,
            cost_estimate=cost(4 * N * CHUNK, 8 * N * CHUNK),
            name=f"relay_{turn}",
        )(
            *[piece[2] for piece in pieces[:count]],
            *[piece[3] for piece in pieces[:count]],
            *got,
        )

    def carried(chunk, candidates, spread, part_x, part_b, part_c, grads):
        place = max(i for i, start in enumerate(starts) if start <= chunk)
        own = pieces[place]
        last = chunk % per_group == per_group - 1
        out_shape = [jax.ShapeDtypeStruct((tokens, row_width), BF16)]
        out_specs = [ANYWHERE]
        scratch = [pltpu.VMEM((tokens, CHUNK), BF16)]
        if last:
            out_shape += [jax.ShapeDtypeStruct((tokens, groups * N), BF16)] * 2
            out_specs += [ANYWHERE] * 2
            scratch += [pltpu.VMEM((tokens, N), BF16)] * 2
        else:
            out_shape += [pltpu.VMEM((tokens, N), F32)] * 2
            out_specs += [IN_VMEM] * 2
        inputs = [*candidates, own[0], own[1], saved_b, own[3], spread, part_x, part_b, part_c]
        aliases = {}
        if grads[0] is not None:
            aliases[len(inputs)] = 0
            inputs.append(grads[0])
        if last and grads[1] is not None:
            for slot in (1, 2):
                aliases[len(inputs)] = slot
                inputs.append(grads[slot])
        results = pl.pallas_call(
            partial(
                carried_kernel,
                chunk=chunk,
                per_group=per_group,
                last=last,
                ranks=ranks,
                start=starts[place],
            ),
            in_specs=[IN_VMEM] * (ranks + 7) + [ANYWHERE] * len(aliases),
            out_specs=out_specs,
            out_shape=out_shape,
            scratch_shapes=scratch + [pltpu.SemaphoreType.DMA((6,))],
            input_output_aliases=aliases,
            compiler_params=PARAMS,
            cost_estimate=cost(6 * tokens * CHUNK * N, 14 * tokens * CHUNK),
            name=f"carried_{chunk}",
        )(*inputs)
        if last:
            return None, list(results)
        return results[1:], [results[0]] + list(grads[1:])

    def links(turn, even_links):
        pairs = []
        for low in range(0 if even_links else 1, ranks - 1, 2):
            if 0 <= turn - low < chunks:
                pairs.append((low, low + 1))
            if 0 <= turn - (ranks - 2 - low) < chunks:
                pairs.append((low + 1, low))
        return pairs

    turns = chunks + ranks - 2
    order = []
    for base in range(turns):
        for turn in (base, base + 1):
            even_links = base % 2 == 0
            if turn < turns and links(turn, even_links):
                order.append((turn, even_links))
    got, parts = {}, {}
    sums, grads = None, [None, None, None]
    groups_left, chunks_left = list(range(groups)), list(range(chunks))

    def carry():
        nonlocal sums, grads
        chunk = chunks_left.pop(0)
        candidates = [got[chunk + hop, hop % 2 == 0] for hop in range(ranks - 1)]
        part_x, part_b, part_c, spread = parts[chunk // per_group]
        if chunk % per_group > 0:
            part_b, part_c = sums
        sums, grads = carried(chunk, candidates, spread, part_x, part_b, part_c, grads)

    for position, (turn, even_links) in enumerate(order):
        before = got.get((turn - 1, not even_links))
        send = first_send if position == 0 else relay(turn, even_links, before)
        key = (turn, even_links)
        got[key] = lax.ppermute(send, "ctx", links(turn, even_links))
        ready = order[: position - 1]
        following = order[position - 1] if position else None
        if position == 1:
            while len(pieces) < len(starts):
                more_states(lax.optimization_barrier((wd, send))[0])
                pieces[-1], got[following] = lax.optimization_barrier(
                    (pieces[-1], got[following])
                )
        elif position % 2 == 0 and position > 0:
            if groups_left and position >= min(4, len(order) - 2):
                held = lax.optimization_barrier((wx, before))[0]
                while groups_left:
                    group = groups_left.pop(0)
                    parts[group] = within(group, held)
                    parts[group], got[following] = lax.optimization_barrier(
                        (parts[group], got[following])
                    )
            elif not groups_left and (chunks_left[0] + ranks - 2, True) in ready:
                carry()
                grads[0], got[following] = lax.optimization_barrier((grads[0], got[following]))
    while groups_left:
        group = groups_left.pop(0)
        parts[group] = within(group, wx)
    while chunks_left:
        carry()
    return tuple(grads)


def solution(mesh):
    rows_cols = P(("groups", "ctx"), ("dp", "inner"))
    return jax.shard_map(
        on_device,
        mesh=mesh,
        in_specs=(rows_cols,) * 5 + (P(("dp", "inner")),) * 2,
        out_specs=(rows_cols,) * 3,
        check_vma=False,
    )
```

```python
from functools import partial

import jax
import jax.numpy as jnp
from jax import lax
from jax.experimental import pallas as pl
from jax.experimental.pallas import tpu as pltpu
from jax.sharding import PartitionSpec as P

P_SIZE = 64
N = 256
CHUNK = 512
CHUNK_HEADS = CHUNK // P_SIZE
F32 = jnp.float32
BF16 = jnp.bfloat16
PARAMS = pltpu.CompilerParams(vmem_limit_bytes=16 * 1024 * 1024)
RELAY_PARAMS = pltpu.CompilerParams(vmem_limit_bytes=4 * 1024 * 1024)
ANYWHERE = pl.BlockSpec(memory_space=pl.ANY)
IN_VMEM = pl.BlockSpec(memory_space=pltpu.VMEM)


def dot(left, right, left_dim, right_dim):
    return lax.dot_general(
        left, right, (((left_dim,), (right_dim,)), ((), ())), preferred_element_type=F32
    )


def terms(value, count):
    parts = []
    for _ in range(count):
        part = value.astype(BF16)
        parts.append(part)
        value = value - part.astype(F32)
    return parts


def head_spread(parts, chunk):
    head_count = parts[0].shape[0]
    shape = (len(parts) * head_count, CHUNK)
    head = lax.rem(lax.broadcasted_iota(jnp.int32, shape, 0), head_count)
    cols = lax.broadcasted_iota(jnp.int32, shape, 1)
    pick = (head == chunk * CHUNK_HEADS + cols // P_SIZE).astype(F32).astype(BF16)
    return dot(jnp.concatenate(parts, axis=0), pick, 0, 0)


def lower_mask(tokens):
    rows = lax.broadcasted_iota(jnp.int32, (tokens, tokens), 0)
    cols = lax.broadcasted_iota(jnp.int32, (tokens, tokens), 1)
    return rows >= cols


def columns(row):
    size = row.shape[1]
    rows = lax.broadcasted_iota(jnp.int32, (size, size), 0)
    cols = lax.broadcasted_iota(jnp.int32, (size, size), 1)
    return jnp.sum(jnp.where(rows == cols, row, 0.0), axis=1, keepdims=True)


def heading(even_links, ranks):
    rank = lax.axis_index("ctx")
    forward = (lax.rem(rank, 2) == 0) == even_links
    return forward, jnp.where(forward, rank, ranks - 1 - rank)


def upper_ones(tokens):
    rows = lax.broadcasted_iota(jnp.int32, (tokens, tokens), 0)
    cols = lax.broadcasted_iota(jnp.int32, (tokens, tokens), 1)
    return (rows <= cols).astype(F32).astype(BF16)


def first_kernel(step_hbm, rate_hbm, dy, x, b, c, send, step, rate, rows_in, group_in, sems, *, ranks):
    rank = lax.axis_index("ctx")

    def fetch(source, target, place):
        if source.shape != target.shape:
            source = source.at[:, pl.ds(0, target.shape[1])]
        copy = pltpu.make_async_copy(source, target, sems.at[place])
        copy.start()
        return copy

    def state(wide, narrow, weigh):
        tokens = step.shape[1]
        halves = [pl.ds(0, tokens // 2), pl.ds(tokens // 2, tokens // 2)]
        copies = [fetch(step_hbm, step, 0), fetch(rate_hbm, rate, 1)]
        copies.append(fetch(narrow, group_in, 2))
        for place, half in enumerate(halves):
            copies.append(fetch(wide.at[half], rows_in.at[half], 3 + place))
        upper = upper_ones(tokens)
        copies[0].wait()
        copies[1].wait()
        cum = dot(step[...], upper, 1, 0) * columns(rate[...])
        spread = head_spread(terms(weigh(cum), 2), 0)
        copies[2].wait()
        total = None
        for place, half in enumerate(halves):
            copies[3 + place].wait()
            low, high = place * (tokens // 2), (place + 1) * (tokens // 2)
            rows = (spread[low:high] * rows_in[half].astype(F32)).astype(BF16)
            part = dot(group_in[half], rows, 0, 0)
            total = part if total is None else total + part
        send[...] = total.astype(BF16)

    @pl.when(rank == 0)
    def _():
        state(x, b, lambda cum: jnp.exp(cum[:, -1:] - cum) * step[...].astype(F32))

    @pl.when(rank == ranks - 1)
    def _():
        state(dy, c, jnp.exp)


def local_kernel(*refs, first, last, per_group):
    if first == 0:
        step_hbm, rate_hbm, dy, x, b, c = refs[:6]
        dyw, xw, states, decay, wd, wx = refs[6:12]
        step, rate, dy_in, x_in, b_in, c_in, sems = refs[12:]
    else:
        wd, wx, dy, x, b, c = refs[:6]
        dyw, xw, states, decay = refs[6:10]
        dy_in, x_in, b_in, c_in, sems = refs[10:]
    tokens = dy_in.shape[0]
    low_group = first // per_group

    def fetch(source, target, place):
        copy = pltpu.make_async_copy(source, target, sems.at[place])
        copy.start()
        return copy

    def part(source, target, low, place):
        return fetch(source.at[:, pl.ds(low, target.shape[1])], target, place)

    if first == 0:
        small = [fetch(step_hbm, step, 4), fetch(rate_hbm, rate, 5)]
    copies = [
        part(dy, dy_in, first * CHUNK, 0),
        part(c, c_in, low_group * N, 1),
        part(x, x_in, first * CHUNK, 2),
        part(b, b_in, low_group * N, 3),
    ]
    if first == 0:
        upper = upper_ones(tokens)
        for copy in small:
            copy.wait()
        cum = dot(step[...], upper, 1, 0) * columns(rate[...])
        wd[0], wd[1] = terms(jnp.exp(cum), 2)
        wx[0], wx[1] = terms(jnp.exp(-cum) * step[...].astype(F32), 2)
    for copy in copies:
        copy.wait()
    for chunk in range(first, last):
        place = chunk - first
        span = pl.ds(place * CHUNK, CHUNK)
        group = pl.ds((chunk // per_group - low_group) * N, N)
        spread = head_spread((wd[0], wd[1]), chunk)
        end = spread[tokens - 1 : tokens, :]
        decay[place] = end
        dyw[:, span] = (spread * dy_in[:, span].astype(F32)).astype(BF16)
        spread = head_spread((wx[0], wx[1]), chunk)
        xw[:, span] = (spread * x_in[:, span].astype(F32)).astype(BF16)
        states[place, 1] = dot(c_in[:, group], dyw[:, span], 0, 0)
        states[place, 0] = dot(b_in[:, group], xw[:, span], 0, 0) * end


def piece(refs, chunk, starts):
    place = max(i for i, start in enumerate(starts) if start <= chunk)
    return refs[place][:, pl.ds((chunk - starts[place]) * CHUNK, CHUNK)]


def within_kernel(*refs, group, per_group, starts):
    count = len(starts)
    dyw, xw, refs = refs[:count], refs[count : 2 * count], refs[2 * count :]
    b, c, dy, wx, gain, grad_x, grad_b, grad_c, spread_out = refs
    lower = lower_mask(b.shape[0])
    own = pl.ds(group * N, N)
    chunks = range(group * per_group, (group + 1) * per_group)
    scores = jnp.where(lower, dot(c[:, own], b[:, own], 1, 1), 0.0).astype(BF16)
    weighted = sum(
        dot(piece(dyw, chunk, starts), piece(xw, chunk, starts), 1, 1) for chunk in chunks
    )
    weighted = jnp.where(lower, weighted, 0.0).astype(BF16)
    grad_b[...] = dot(weighted, c[:, own], 0, 0)
    grad_c[...] = dot(weighted, b[:, own], 1, 0)
    gains = terms(jnp.broadcast_to(columns(gain[...]), (gain.shape[1], 128)), 3)
    for part, chunk in enumerate(chunks):
        spread = head_spread((wx[0], wx[1]), chunk)
        rows = dy[:, pl.ds(chunk * CHUNK, CHUNK)].astype(F32)
        skip = head_spread(gains, chunk)[0:1, :] * rows
        spread_out[:, pl.ds(part * CHUNK, CHUNK)] = spread
        grad_x[:, pl.ds(part * CHUNK, CHUNK)] = (
            spread * dot(scores, piece(dyw, chunk, starts), 0, 0) + skip
        )


def relay_kernel(*refs, turn, even_links, ranks, starts):
    out, refs = refs[-1], refs[:-1]
    count = len(starts)
    states, decays, got = refs[:count], refs[count : 2 * count], refs[2 * count :]
    forward, lag = heading(even_links, ranks)
    kind = jnp.where(forward, 0, 1)
    chunk = turn - lag
    state = shrink = None
    for start, state_ref, decay_ref in zip(starts, states, decays):
        place = jnp.clip(chunk - start, 0, state_ref.shape[0] - 1)
        if state is None:
            state, shrink = state_ref[place, kind], decay_ref[place]
        else:
            state = jnp.where(chunk >= start, state_ref[place, kind], state)
            shrink = jnp.where(chunk >= start, decay_ref[place], shrink)
    if got:
        state = got[0][...].astype(F32) * shrink + state
    out[...] = state.astype(BF16)


def chosen(candidates, source):
    value = jnp.zeros(candidates[0].shape, BF16)
    for place, candidate in enumerate(candidates):
        value = jnp.where(source == place, candidate[...], value)
    return value


def carried_kernel(*refs, chunk, per_group, last, ranks, start):
    rank = lax.axis_index("ctx")
    fwd_in = chosen(refs[: ranks - 1], rank - 1)
    back_in = chosen(refs[: ranks - 1], ranks - 2 - rank)
    refs = refs[ranks - 1 :]
    dyw, xw, b, decay, spread, part_x, part_b, part_c = refs[:8]
    group, inside = chunk // per_group, chunk % per_group
    grad_x, grad_b, grad_c = refs[-7 if last else -5 :][:3]
    x_out = refs[-4] if last else refs[-2]
    sems = refs[-1]
    place = chunk - start
    span = pl.ds(place * CHUNK, CHUNK)
    own = pl.ds(group * N, N)
    copies = []

    def send(source, target, place):
        copies.append(pltpu.make_async_copy(source, target, sems.at[place]))
        copies[-1].start()

    back = (back_in.astype(F32) * decay[place]).astype(BF16)
    part = pl.ds(inside * CHUNK, CHUNK)
    half = b.shape[0] // 2
    for low in (0, half):
        rows = pl.ds(low, half)
        slot = 3 * (low > 0)
        carried = spread[rows, part] * dot(b[rows, own], back, 1, 0)
        x_out[rows] = (part_x[rows, part] + carried).astype(BF16)
        send(x_out.at[rows], grad_x.at[rows, pl.ds(chunk * CHUNK, CHUNK)], slot)
        total_b = part_b[rows] + dot(xw[rows, span], back, 1, 1)
        total_c = part_c[rows] + dot(dyw[rows, span], fwd_in, 1, 1)
        if last:
            b_out, c_out = refs[-3:-1]
            b_out[rows] = total_b.astype(BF16)
            send(b_out.at[rows], grad_b.at[rows, own], slot + 1)
            c_out[rows] = total_c.astype(BF16)
            send(c_out.at[rows], grad_c.at[rows, own], slot + 2)
        else:
            grad_b[rows] = total_b
            grad_c[rows] = total_c
    for copy in copies:
        copy.wait()


def cost(flops, bytes_accessed):
    return pl.CostEstimate(flops=flops, bytes_accessed=bytes_accessed, transcendentals=0)


def on_device(grad_out, saved_x, saved_b, saved_c, step_size, decay_rate, skip_gain):
    tokens, row_width = grad_out.shape
    head_count = step_size.shape[1]
    groups = saved_b.shape[1] // N
    chunks = row_width // CHUNK
    per_group = chunks // groups
    group_width = row_width // groups
    ranks = lax.axis_size("ctx")
    gain_row = skip_gain.reshape(1, head_count)
    stay = partial(pltpu.with_memory_space_constraint, memory_space=pltpu.HBM)
    sources = [stay(array) for array in (grad_out, saved_x, saved_b, saved_c)]
    starts = [start for start in (0, 2) if start < chunks]
    stops = starts[1:] + [chunks]

    def local_states(first, last, inputs, in_spec, extra_shapes, extra_scratch):
        wide = (last - first) * CHUNK
        out_shape = [
            pltpu.VMEM((tokens, wide), BF16),
            pltpu.VMEM((tokens, wide), BF16),
            pltpu.VMEM((last - first, 2, N, CHUNK), F32),
            pltpu.VMEM((last - first, 1, CHUNK), F32),
        ] + extra_shapes
        tall = ((last - 1) // per_group - first // per_group + 1) * N
        return pl.pallas_call(
            partial(local_kernel, first=first, last=last, per_group=per_group),
            in_specs=[in_spec] * 2 + [ANYWHERE] * 4,
            out_specs=[IN_VMEM] * len(out_shape),
            out_shape=out_shape,
            scratch_shapes=extra_scratch
            + [
                pltpu.VMEM((tokens, wide), BF16),
                pltpu.VMEM((tokens, wide), BF16),
                pltpu.VMEM((tokens, tall), BF16),
                pltpu.VMEM((tokens, tall), BF16),
                pltpu.SemaphoreType.DMA((6,)),
            ],
            compiler_params=PARAMS,
            cost_estimate=cost(4 * tokens * wide * (N + 512), 6 * tokens * wide),
            name=f"states_{first}",
        )(*inputs)

    small_scratch = [
        pltpu.VMEM((head_count, tokens), BF16),
        pltpu.VMEM((1, head_count), F32),
    ]
    step_rows, rate_row = step_size.T, decay_rate.reshape(1, head_count)
    first_send = pl.pallas_call(
        partial(first_kernel, ranks=ranks),
        in_specs=[ANYWHERE] * 6,
        out_specs=IN_VMEM,
        out_shape=pltpu.VMEM((N, CHUNK), BF16),
        scratch_shapes=small_scratch
        + [
            pltpu.VMEM((tokens, CHUNK), BF16),
            pltpu.VMEM((tokens, N), BF16),
            pltpu.SemaphoreType.DMA((5,)),
        ],
        compiler_params=PARAMS,
        cost_estimate=cost(2 * tokens * CHUNK * (N + 256), 4 * tokens * CHUNK),
        name="first_state",
    )(stay(step_rows), stay(rate_row), *sources)
    rate_row, _ = lax.optimization_barrier((rate_row, first_send))
    *head, wd, wx = local_states(
        0,
        stops[0],
        [stay(step_rows), stay(rate_row)] + sources,
        ANYWHERE,
        [pltpu.VMEM((2, head_count, tokens), BF16)] * 2,
        small_scratch,
    )
    pieces = [head]

    def more_states(wd):
        place = len(pieces)
        pieces.append(
            local_states(
                starts[place], stops[place], [wd, wx] + sources, IN_VMEM, [], []
            )
        )

    def within(group, wx):
        return pl.pallas_call(
            partial(within_kernel, group=group, per_group=per_group, starts=starts),
            in_specs=[IN_VMEM] * (2 * len(starts) + 5),
            out_specs=[IN_VMEM] * 4,
            out_shape=[
                pltpu.VMEM((tokens, group_width), F32),
                pltpu.VMEM((tokens, N), F32),
                pltpu.VMEM((tokens, N), F32),
                pltpu.VMEM((tokens, group_width), F32),
            ],
            compiler_params=PARAMS,
            cost_estimate=cost(
                4 * tokens * tokens * (group_width + 2 * N), 10 * tokens * group_width
            ),
            name=f"within_{group}",
        )(
            *[piece[0] for piece in pieces],
            *[piece[1] for piece in pieces],
            saved_b,
            saved_c,
            grad_out,
            wx,
            gain_row,
        )

    def relay(turn, even_links, got):
        top = turn if even_links else turn - 1
        count = sum(start <= top for start in starts)
        got = [] if got is None else [got]
        return pl.pallas_call(
            partial(
                relay_kernel,
                turn=turn,
                even_links=even_links,
                ranks=ranks,
                starts=starts[:count],
            ),
            in_specs=[IN_VMEM] * (2 * count + len(got)),
            out_specs=IN_VMEM,
            out_shape=pltpu.VMEM((N, CHUNK), BF16),
            compiler_params=RELAY_PARAMS,
            cost_estimate=cost(4 * N * CHUNK, 8 * N * CHUNK),
            name=f"relay_{turn}",
        )(
            *[piece[2] for piece in pieces[:count]],
            *[piece[3] for piece in pieces[:count]],
            *got,
        )

    def carried(chunk, candidates, spread, part_x, part_b, part_c, grads):
        place = max(i for i, start in enumerate(starts) if start <= chunk)
        own = pieces[place]
        last = chunk % per_group == per_group - 1
        out_shape = [jax.ShapeDtypeStruct((tokens, row_width), BF16)]
        out_specs = [ANYWHERE]
        scratch = [pltpu.VMEM((tokens, CHUNK), BF16)]
        if last:
            out_shape += [jax.ShapeDtypeStruct((tokens, groups * N), BF16)] * 2
            out_specs += [ANYWHERE] * 2
            scratch += [pltpu.VMEM((tokens, N), BF16)] * 2
        else:
            out_shape += [pltpu.VMEM((tokens, N), F32)] * 2
            out_specs += [IN_VMEM] * 2
        inputs = [*candidates, own[0], own[1], saved_b, own[3], spread, part_x, part_b, part_c]
        aliases = {}
        if grads[0] is not None:
            aliases[len(inputs)] = 0
            inputs.append(grads[0])
        if last and grads[1] is not None:
            for slot in (1, 2):
                aliases[len(inputs)] = slot
                inputs.append(grads[slot])
        results = pl.pallas_call(
            partial(
                carried_kernel,
                chunk=chunk,
                per_group=per_group,
                last=last,
                ranks=ranks,
                start=starts[place],
            ),
            in_specs=[IN_VMEM] * (ranks + 7) + [ANYWHERE] * len(aliases),
            out_specs=out_specs,
            out_shape=out_shape,
            scratch_shapes=scratch + [pltpu.SemaphoreType.DMA((6,))],
            input_output_aliases=aliases,
            compiler_params=PARAMS,
            cost_estimate=cost(6 * tokens * CHUNK * N, 14 * tokens * CHUNK),
            name=f"carried_{chunk}",
        )(*inputs)
        if last:
            return None, list(results)
        return results[1:], [results[0]] + list(grads[1:])

    def links(turn, even_links):
        pairs = []
        for low in range(0 if even_links else 1, ranks - 1, 2):
            if 0 <= turn - low < chunks:
                pairs.append((low, low + 1))
            if 0 <= turn - (ranks - 2 - low) < chunks:
                pairs.append((low + 1, low))
        return pairs

    turns = chunks + ranks - 2
    order = []
    for base in range(turns):
        for turn in (base, base + 1):
            even_links = base % 2 == 0
            if turn < turns and links(turn, even_links):
                order.append((turn, even_links))
    got, parts = {}, {}
    sums, grads = None, [None, None, None]
    groups_left, chunks_left = list(range(groups)), list(range(chunks))

    def carry():
        nonlocal sums, grads
        chunk = chunks_left.pop(0)
        candidates = [got[chunk + hop, hop % 2 == 0] for hop in range(ranks - 1)]
        part_x, part_b, part_c, spread = parts[chunk // per_group]
        if chunk % per_group > 0:
            part_b, part_c = sums
        sums, grads = carried(chunk, candidates, spread, part_x, part_b, part_c, grads)

    for position, (turn, even_links) in enumerate(order):
        before = got.get((turn - 1, not even_links))
        send = first_send if position == 0 else relay(turn, even_links, before)
        key = (turn, even_links)
        got[key] = lax.ppermute(send, "ctx", links(turn, even_links))
        ready = order[: position - 1]
        following = order[position - 1] if position else None
        if position == 1:
            while len(pieces) < len(starts):
                more_states(lax.optimization_barrier((wd, send))[0])
                pieces[-1], got[following] = lax.optimization_barrier(
                    (pieces[-1], got[following])
                )
        elif position % 2 == 0 and position > 0:
            if groups_left and position >= min(4, len(order) - 2):
                held = lax.optimization_barrier((wx, before))[0]
                while groups_left:
                    group = groups_left.pop(0)
                    parts[group] = within(group, held)
                    parts[group], got[following] = lax.optimization_barrier(
                        (parts[group], got[following])
                    )
            elif not groups_left and (chunks_left[0] + ranks - 2, True) in ready:
                carry()
                grads[0], got[following] = lax.optimization_barrier((grads[0], got[following]))
    while groups_left:
        group = groups_left.pop(0)
        parts[group] = within(group, wx)
    while chunks_left:
        carry()
    return tuple(grads)


def solution(mesh):
    rows_cols = P(("groups", "ctx"), ("dp", "inner"))
    return jax.shard_map(
        on_device,
        mesh=mesh,
        in_specs=(rows_cols,) * 5 + (P(("dp", "inner")),) * 2,
        out_specs=(rows_cols,) * 3,
        check_vma=False,
    )
```
